32 devices in a mesh: row: 8 (over z, x), col: 4 (over y, core).
Axes of the slice: x: 2, y: 2, z: 4, core: 2. Of those that a mesh axis runs over, the one named last changes fastest.
Arguments:
- amp_tiles: bfloat16 [2, 4, 32, 256, 256], P(None, 'col', 'row'), may hold values from -6 to 6
- amp_rows: int32 [2, 4, 32], P(None, 'col', 'row'), may hold values from -1 to 3, as said below
- int_tiles: bfloat16 [2, 8, 8, 256, 256], P(None, 'col', 'row'), may hold values from -0.1875 to 0.1875
- int_codes: int32 [2, 8, 8], P(None, 'col', 'row'), may hold values from -1 to 11, as said below
Outputs:
- ladder: float32 [4096, 12288], P('col', 'row')
The draws below stay inside these ranges and needn't reach their ends.
Inputs may be any that keep to these rules, and one draw needn't show every extreme that they name: `amp_rows`: the live tile rows among one device's 4 amplitude slots of a panel are distinct; -1 marks an empty slot. `int_codes`: the live codes among one device's 2 integral slots of a panel are distinct; -1 marks an empty slot.
All inputs are finite; a program needn't handle non-finite values.
Results may differ from the reference program's by a relative error of at most 0.0003.
Values may be sent and summed in bfloat16 or wider, within the bound.
No kernel may reach another device: no remote copies, remote signals or barrier semaphores. Data moves between devices by JAX's collectives and lax.ppermute only.
A program may use at most 192 MiB of HBM per device.

```python
import jax
import jax.numpy as jnp
from jax import lax

TL = 256
MI = 4
NJ = 6
SA = 4
SB = 2
STEPS = 2
KB = 2
N_ROW = 8
N_COL = 4


def distinct_pick(key, lead_shape, span_size, pick_count):
    scores = jax.random.randint(key, lead_shape + (span_size,), 0, 1 << 20) * span_size + jnp.arange(span_size, dtype=jnp.int32)
    ranking = jnp.argsort(scores, axis=-1, stable=True).astype(jnp.int32)
    picked = ranking[..., :pick_count]
    vacant = jax.random.randint(jax.random.fold_in(key, 7), lead_shape + (pick_count,), 0, 4) == 0
    return jnp.where(vacant, -1, picked).astype(jnp.int32)


def draw_amp_rows(key, part):
    picked = distinct_pick(jax.random.fold_in(key, 11), (STEPS, N_COL, N_ROW), MI, SA)
    return picked.reshape(STEPS, N_COL, N_ROW * SA)


def draw_int_codes(key, part):
    picked = distinct_pick(jax.random.fold_in(key, 23), (STEPS, N_COL, N_ROW), KB * NJ, SB)
    return jnp.transpose(picked, (0, 1, 3, 2)).reshape(STEPS, N_COL * SB, N_ROW)


def block_scale(rng, extent, shards, low, top_value):
    loudness, own = 1.0, jax.random.fold_in(rng, 6)
    for axis_at, shards_of in shards:
        heights = jnp.exp(jax.random.uniform(jax.random.fold_in(own, axis_at), (shards_of,), jnp.float32, low / len(shards), top_value / len(shards)))
        loudness = loudness * jnp.repeat(heights, extent[axis_at] // shards_of).reshape([-1 if axis == axis_at else 1 for axis in range(len(extent))])
    return loudness


def bell_draw(rng, dims, spread, most, pieces=(), held_as=jnp.bfloat16):
    level = block_scale(rng, dims, pieces, -0.22, 0.18) if pieces else 1.0
    values = jax.random.normal(rng, dims, jnp.float32) * spread * level
    return jnp.minimum(jnp.maximum(values, -most), most).astype(held_as)


def setup_inputs(seed: int = 0) -> dict:
    key_of = jax.random.split(jax.random.key(seed), 5)
    amp_tiles = bell_draw(key_of[0], (STEPS, N_COL, N_ROW * SA, TL, TL), 1.0, 6.0, ((1, 4), (2, 8)))
    amp_rows = draw_amp_rows(jax.random.fold_in(key_of[4], 71), 0)
    int_tiles = bell_draw(key_of[2], (STEPS, N_COL * SB, N_ROW, TL, TL), (TL * 4) ** -0.5, 0.1875, ((1, 4), (2, 8)))
    int_codes = draw_int_codes(jax.random.fold_in(key_of[4], 71), 0)
    return {"amp_tiles": amp_tiles, "amp_rows": amp_rows, "int_tiles": int_tiles, "int_codes": int_codes}


def densify(tiles, codes, per_dev, rows_held, panel_tiles, cols_tiles, width):
    slot_ids = jnp.arange(codes.shape[0], dtype=jnp.int32)
    living = codes >= 0
    k_index = jnp.where(living, (slot_ids // per_dev) * rows_held + codes // cols_tiles, panel_tiles).astype(jnp.int32)
    j_index = jnp.where(living, codes % cols_tiles, 0).astype(jnp.int32)
    dense = jnp.zeros((panel_tiles, width, cols_tiles, width), jnp.bfloat16)
    dense = dense.at[k_index, :, j_index, :].set(tiles, mode="drop")
    return dense.reshape(panel_tiles, width, cols_tiles * width)


def reference(amp_tiles, amp_rows, int_tiles, int_codes):
    total = jnp.zeros((N_COL, MI, TL, N_ROW, NJ * TL), jnp.float32)
    for step in range(STEPS):
        panels = jnp.stack([densify(int_tiles[step, :, rank], int_codes[step, :, rank], SB, KB, N_ROW, NJ, TL) for rank in range(N_ROW)])

        def per_col(items):
            tiles, rows = items

            def one_slot(carry, item):
                tile, tile_rows, slot = item
                k_index = (slot // SA).astype(jnp.int32)
                block = lax.dynamic_index_in_dim(panels, k_index, 1, keepdims=False).astype(jnp.float32)
                product = jnp.einsum("xy,ryz->xrz", tile.astype(jnp.float32), block, precision=lax.Precision.HIGHEST)
                living = (tile_rows >= 0).astype(jnp.float32)
                target = jnp.maximum(tile_rows, 0).astype(jnp.int32)
                current = lax.dynamic_index_in_dim(carry, target, 0, keepdims=False)
                return lax.dynamic_update_index_in_dim(carry, current + living * product, target, 0), None

            start_total = jnp.zeros((MI, TL, N_ROW, NJ * TL), jnp.float32)
            slot_ids = jnp.arange(rows.shape[0], dtype=jnp.int32)
            result, _ = lax.scan(one_slot, start_total, (tiles, rows, slot_ids))
            return result

        total = total + lax.map(per_col, (amp_tiles[step], amp_rows[step]))
    return total.reshape(N_COL * MI * TL, N_ROW * NJ * TL)
```

```python
import functools

import jax
import jax.numpy as jnp
from jax import lax
from jax.experimental import pallas as pl
from jax.experimental.pallas import tpu as pltpu
from jax.sharding import PartitionSpec as P

MI = 4
NJ = 6
CORES = 2
GROUPS = ((0, 2), (2, 4))
VMEM_LIMIT = 8 * 1024 * 1024


def grid_cycle(depth, across):
    order = [z * across for z in range(depth)]
    for turn, z in enumerate(reversed(range(depth))):
        xs = range(1, across) if turn % 2 == 0 else range(across - 1, 0, -1)
        order += [z * across + x for x in xs]
    return order


def pick(table, index):
    value = jnp.int32(table[0])
    for at in range(1, len(table)):
        value = jnp.where(index == at, jnp.int32(table[at]), value)
    return value


def place_kernel(rows_ref, tiles_ref, *rest):
    placed, sem = rest[:-1], rest[-1]
    panels, slots, width = tiles_ref.shape[0], tiles_ref.shape[2], tiles_ref.shape[3]
    jobs = []
    for group, (first, last) in enumerate(GROUPS):
        for panel in range(panels):
            ref = placed[group * panels + panel]
            for row in range(first, last):
                slot = jnp.int32(-1)
                for at in range(slots):
                    slot = jnp.where(rows_ref[panel, 0, at] == row, at, slot)
                spot = ref.at[pl.ds((row - first) * width, width)]
                copy = pltpu.make_async_copy(
                    tiles_ref.at[panel, 0, jnp.maximum(slot, 0)], spot, sem.at[panel, row]
                )
                jobs.append((slot, spot, copy))
    for slot, spot, copy in jobs:

        @pl.when(slot >= 0)
        def _():
            copy.start()

        @pl.when(slot < 0)
        def _():
            spot[...] = jnp.zeros(spot.shape, spot.dtype)

    for slot, spot, copy in jobs:

        @pl.when(slot >= 0)
        def _():
            copy.wait()


def place(amp_tiles, amp_rows):
    panels, width = amp_tiles.shape[0], amp_tiles.shape[3]
    shapes = [
        pltpu.VMEM(((last - first) * width, width), amp_tiles.dtype)
        for first, last in GROUPS
        for _ in range(panels)
    ]
    return pl.pallas_call(
        place_kernel,
        out_shape=shapes,
        in_specs=[pl.BlockSpec(memory_space=pltpu.SMEM), pl.BlockSpec(memory_space=pl.ANY)],
        out_specs=[pl.BlockSpec(memory_space=pltpu.VMEM)] * len(shapes),
        scratch_shapes=[pltpu.SemaphoreType.DMA((panels, MI))],
        compiler_params=pltpu.CompilerParams(vmem_limit_bytes=VMEM_LIMIT),
        name="place",
    )(amp_rows, amp_tiles)


def collect_kernel(*refs):
    parts, out_ref, sem = refs[:-2], refs[-2], refs[-1]
    panels, slots = parts[0].shape[0], parts[0].shape[1]
    count = len(parts)
    col = lax.axis_index("col")
    y, core = col // CORES, lax.rem(col, CORES)
    depth = count // CORES
    copies = []
    for at, part in enumerate(parts):
        shift, flip = at // CORES, at % CORES
        owner = lax.rem(y + depth - shift, depth) * CORES + lax.rem(core + flip, CORES)
        for panel in range(panels):
            copies.append(
                pltpu.make_async_copy(
                    part.at[panel], out_ref.at[panel, pl.ds(owner * slots, slots)], sem.at[at, panel]
                )
            )
    for copy in copies:
        copy.start()
    for copy in copies:
        copy.wait()


def collect(parts):
    panels, slots, width, _ = parts[0].shape
    return pl.pallas_call(
        collect_kernel,
        out_shape=pltpu.VMEM((panels, slots * len(parts), width, width), parts[0].dtype),
        in_specs=[pl.BlockSpec(memory_space=pl.ANY)] * len(parts),
        out_specs=pl.BlockSpec(memory_space=pltpu.VMEM),
        scratch_shapes=[pltpu.SemaphoreType.DMA((len(parts), panels))],
        compiler_params=pltpu.CompilerParams(vmem_limit_bytes=VMEM_LIMIT),
        name="collect",
    )(*parts)


def chunk_updates(codes_ref, hops, order, rows_held, slots):
    me = lax.axis_index("row")
    inverse = [order.index(at) for at in range(len(order))]
    here = pick(inverse, me)
    found = []
    for panel, hop in hops:
        way = hop if panel % 2 == 0 else len(order) - hop
        source = pick(order, lax.rem(here + len(order) - way, len(order)))
        owner, held = source // rows_held, lax.rem(source, rows_held)
        for at in range(slots):
            slot = owner * slots + at
            code = codes_ref[panel, slot, 0]
            live = (code >= 0) & (code // NJ == held)
            found.append((live, slot, lax.rem(jnp.maximum(code, 0), NJ)))
    return found


def fold_kernel(first, last, hops, order, rows_held, slots, band, codes_ref, ints_ref, *refs):
    chunks = refs[: len(hops)]
    width = ints_ref.shape[2]
    if first:
        total_ref = refs[len(hops)]
        total_ref[...] = jnp.zeros(total_ref.shape, jnp.float32)
    elif last:
        total_ref, out_ref, sem = refs[len(hops)], refs[-2], refs[-1]
    else:
        total_ref = refs[-1]
    found = chunk_updates(codes_ref, hops, order, rows_held, slots)

    def send(column):
        cols = pl.ds(column * width, width)
        return pltpu.make_async_copy(
            total_ref.at[:, cols],
            out_ref.at[pl.ds(band[0], band[1]), cols],
            sem.at[column],
        )

    touched = []
    if last:
        for column in range(NJ):
            hit = False
            for live, _, at in found:
                hit = hit | (live & (at == column))
            touched.append(hit)

            @pl.when(jnp.logical_not(hit))
            def _():
                send(column).start()

    for index, (live, slot, column) in enumerate(found):
        panel, chunk = hops[index // slots][0], chunks[index // slots]

        @pl.when(live)
        def _():
            cols = pl.ds(pl.multiple_of(column * width, width), width)
            total_ref[:, cols] += jnp.dot(
                chunk[...], ints_ref[panel, slot], preferred_element_type=jnp.float32
            )

    if last:
        for column in range(NJ):

            @pl.when(touched[column])
            def _():
                send(column).start()

        for column in range(NJ):
            send(column).wait()


def in_vmem(value):
    return pltpu.with_memory_space_constraint(value, pltpu.VMEM)


def fold(codes, ints, chunks, hops, total, order, rows_held, slots, band, out=None, whole=None):
    first, last = total is None, whole is not None
    rows, width = chunks[0].shape
    vmem = pl.BlockSpec(memory_space=pltpu.VMEM)
    anywhere = pl.BlockSpec(memory_space=pl.ANY)
    operands = [codes, in_vmem(ints), *map(in_vmem, chunks)]
    in_specs = [pl.BlockSpec(memory_space=pltpu.SMEM)] + [vmem] * (1 + len(chunks))
    aliases, scratch = {}, []
    if not first:
        operands.append(in_vmem(total))
        in_specs.append(vmem)
    if last:
        out_shape, out_spec = jax.ShapeDtypeStruct(whole, jnp.float32), anywhere
        scratch = [pltpu.SemaphoreType.DMA((NJ,))]
        if out is not None:
            aliases = {len(operands): 0}
            operands.append(out)
            in_specs.append(anywhere)
    else:
        out_shape, out_spec = pltpu.VMEM((rows, NJ * width), jnp.float32), vmem
        if not first:
            aliases = {len(operands) - 1: 0}
    return pl.pallas_call(
        functools.partial(fold_kernel, first, last, hops, order, rows_held, slots, band),
        out_shape=out_shape,
        in_specs=in_specs,
        out_specs=out_spec,
        scratch_shapes=scratch,
        input_output_aliases=aliases,
        compiler_params=pltpu.CompilerParams(vmem_limit_bytes=VMEM_LIMIT),
        cost_estimate=pl.CostEstimate(
            flops=2 * rows * width * width * len(hops) * slots, bytes_accessed=rows * NJ * width * 4, transcendentals=0
        ),
        name="fold",
    )(*operands)


def body(amp_tiles, amp_rows, int_tiles, int_codes):
    n_row, n_col = lax.axis_size("row"), lax.axis_size("col")
    rows_held = n_row // n_col
    panels, slots, width = int_tiles.shape[0], int_tiles.shape[1], int_tiles.shape[3]
    across = n_col // CORES
    order = grid_cycle(n_row // across, across)
    forth = [(order[at], order[(at + 1) % n_row]) for at in range(n_row)]
    ways = [forth if panel % 2 == 0 else [(b, a) for a, b in forth] for panel in range(panels)]

    streams = place(amp_tiles, amp_rows)
    rings = []
    held = list(streams)
    rings.append(held)
    for _ in range(1, n_row):
        held = [lax.ppermute(held[at], "row", ways[at % panels]) for at in range(len(held))]
        rings.append(held)

    codes = lax.all_gather(int_codes, "col", axis=1, tiled=True)
    own = int_tiles.reshape(panels, slots, width, width)
    flip = [(c, c // CORES * CORES + (c + 1) % CORES) for c in range(n_col)]
    parts = []
    for shift in range(n_col // CORES):
        moved = own
        if shift:
            moved = lax.ppermute(own, "col", [(c, (c + shift * CORES) % n_col) for c in range(n_col)])
        parts += [moved, lax.ppermute(moved, "col", flip)]
    ints = collect(parts)

    whole = (MI * width, NJ * width)
    cuts = [0, n_row // 2, n_row - 1, n_row]
    totals = [None] * len(GROUPS)
    out = None
    for begin, end in zip(cuts[:-1], cuts[1:]):
        hops = [(panel, hop) for hop in range(begin, end) for panel in range(panels)]
        for group, (top, bottom) in enumerate(GROUPS):
            chunks = [rings[hop][group * panels + panel] for panel, hop in hops]
            band = (top * width, (bottom - top) * width)
            made = fold(
                codes, ints, chunks, hops, totals[group], order, rows_held, slots, band,
                out, whole if end == n_row else None,
            )
            if end == n_row:
                out = made
            else:
                totals[group] = made
    return out


def solution(mesh):
    return jax.shard_map(
        body,
        mesh=mesh,
        in_specs=(
            P(None, "col", "row", None, None),
            P(None, "col", "row"),
            P(None, "col", "row", None, None),
            P(None, "col", "row"),
        ),
        out_specs=P("col", "row"),
        check_vma=False,
    )
```

```python
import functools

import jax
import jax.numpy as jnp
from jax import lax
from jax.experimental import pallas as pl
from jax.experimental.pallas import tpu as pltpu
from jax.sharding import PartitionSpec as P

MI = 4
NJ = 6
CORES = 2
GROUPS = ((0, 2), (2, 4))
LINES = 16
VMEM_LIMIT = 8 * 1024 * 1024


def grid_cycle(depth, across):
    order = [z * across for z in range(depth)]
    for turn, z in enumerate(reversed(range(depth))):
        xs = range(1, across) if turn % 2 == 0 else range(across - 1, 0, -1)
        order += [z * across + x for x in xs]
    return order


def pick(table, index):
    value = jnp.int32(table[0])
    for at in range(1, len(table)):
        value = jnp.where(index == at, jnp.int32(table[at]), value)
    return value


def in_vmem(value):
    return pltpu.with_memory_space_constraint(value, pltpu.VMEM)


def in_hbm(value):
    return pltpu.with_memory_space_constraint(value, pltpu.HBM)


def place_kernel(rows_hbm, codes_hbm, tiles_hbm, ints_hbm, *rest):
    placed, parcel_ref = rest[: -1 - 6], rest[-1 - 6]
    rows_ref, codes_ref, tiles_ref, small_sem, tiles_sem, ints_sem = rest[-6:]
    panels, slots, width = tiles_ref.shape[0], tiles_ref.shape[1], tiles_ref.shape[2]
    held = ints_hbm.shape[1]
    small = [
        pltpu.make_async_copy(rows_hbm, rows_ref, small_sem.at[0]),
        pltpu.make_async_copy(codes_hbm, codes_ref, small_sem.at[1]),
    ]
    tiles = [
        pltpu.make_async_copy(tiles_hbm.at[panel, 0], tiles_ref.at[panel], tiles_sem.at[panel])
        for panel in range(panels)
    ]
    parcels = [
        pltpu.make_async_copy(
            ints_hbm.at[panel, at, 0],
            parcel_ref.at[pl.ds((panel * held + at) * width, width)],
            ints_sem.at[panel, at],
        )
        for panel in range(panels)
        for at in range(held)
    ]
    for copy in small + tiles + parcels:
        copy.start()
    for copy in small:
        copy.wait()
    lines = lax.broadcasted_iota(jnp.int32, (LINES, width), 0)
    labels = jnp.zeros((LINES, width), jnp.float32)
    for panel in range(panels):
        for at in range(held):
            code = codes_ref[panel, 0, at].astype(jnp.float32)
            labels = jnp.where(lines == panel * held + at, code, labels)
    parcel_ref[pl.ds(panels * held * width, LINES)] = labels.astype(parcel_ref.dtype)
    for panel in range(panels):
        tiles[panel].wait()
        for group, (first, last) in enumerate(GROUPS):
            for row in range(first, last):
                slot = jnp.int32(-1)
                for at in range(slots):
                    slot = jnp.where(rows_ref[panel, 0, at] == row, at, slot)
                spot = placed[group * panels + panel].at[pl.ds((row - first) * width, width)]

                @pl.when(slot >= 0)
                def _():
                    spot[...] = tiles_ref[panel, jnp.maximum(slot, 0)]

                @pl.when(slot < 0)
                def _():
                    spot[...] = jnp.zeros(spot.shape, spot.dtype)

    for copy in parcels:
        copy.wait()


def place(amp_tiles, amp_rows, int_tiles, int_codes):
    panels, held, slots, width = amp_tiles.shape[0], int_tiles.shape[1], amp_tiles.shape[2], amp_tiles.shape[3]
    codes = jnp.transpose(int_codes, (0, 2, 1))
    shapes = [
        pltpu.VMEM(((last - first) * width, width), amp_tiles.dtype)
        for first, last in GROUPS
        for _ in range(panels)
    ]
    shapes.append(pltpu.VMEM((panels * held * width + LINES, width), int_tiles.dtype))
    return pl.pallas_call(
        place_kernel,
        out_shape=shapes,
        in_specs=[pl.BlockSpec(memory_space=pl.ANY)] * 4,
        out_specs=[pl.BlockSpec(memory_space=pltpu.VMEM)] * len(shapes),
        scratch_shapes=[
            pltpu.SMEM(amp_rows.shape, jnp.int32),
            pltpu.SMEM(codes.shape, jnp.int32),
            pltpu.VMEM((panels, slots, width, width), amp_tiles.dtype),
            pltpu.SemaphoreType.DMA((2,)),
            pltpu.SemaphoreType.DMA((panels,)),
            pltpu.SemaphoreType.DMA((panels, held)),
        ],
        compiler_params=pltpu.CompilerParams(vmem_limit_bytes=VMEM_LIMIT),
        name="place",
    )(in_hbm(amp_rows), in_hbm(codes), in_hbm(amp_tiles), in_hbm(int_tiles))


def collect_kernel(panels, slots, base, *refs):
    parts, codes_ref, out_ref = refs[:-2], refs[-2], refs[-1]
    width = parts[0].shape[1]
    col = lax.axis_index("col")
    y, core = col // CORES, lax.rem(col, CORES)
    depth = len(parts) // CORES
    owners = []
    for at, part in enumerate(parts):
        shift, flip = at // CORES, at % CORES
        owner = lax.rem(y + depth - shift, depth) * CORES + lax.rem(core + flip, CORES)
        owners.append(owner)
        for panel in range(panels):
            for slot in range(slots):
                out_ref[panel, owner * slots + slot] = part[pl.ds((panel * slots + slot) * width, width)]
    lines = lax.broadcasted_iota(jnp.int32, (LINES, width), 0)
    scale = jnp.zeros((LINES, width), jnp.float32)
    for at in range(panels * slots):
        scale = jnp.where(lines == at, float(base**at), scale)
    for owner, part in zip(owners, parts):
        labels = part[pl.ds(panels * slots * width, LINES), pl.ds(0, 128)].astype(jnp.float32) + 1.0
        number = jnp.sum(labels * scale[:, :128], axis=0, keepdims=True)
        digits = jnp.max(number).astype(jnp.int32)
        for panel in range(panels):
            for slot in range(slots):
                codes_ref[panel, owner * slots + slot] = lax.rem(digits, base) - 1
                digits = digits // base


def collect(parts, panels, slots, base):
    width = parts[0].shape[1]
    total = slots * len(parts)
    assert base ** (panels * slots) < 2**24
    vmem = pl.BlockSpec(memory_space=pltpu.VMEM)
    return pl.pallas_call(
        functools.partial(collect_kernel, panels, slots, base),
        out_shape=[
            jax.ShapeDtypeStruct((panels, total), jnp.int32),
            pltpu.VMEM((panels, total, width, width), parts[0].dtype),
        ],
        in_specs=[vmem] * len(parts),
        out_specs=[pl.BlockSpec(memory_space=pltpu.SMEM), vmem],
        compiler_params=pltpu.CompilerParams(vmem_limit_bytes=VMEM_LIMIT),
        name="collect",
    )(*map(in_vmem, parts))


def chunk_updates(codes_ref, hops, order, rows_held, slots):
    me = lax.axis_index("row")
    inverse = [order.index(at) for at in range(len(order))]
    here = pick(inverse, me)
    found = []
    for panel, hop in hops:
        way = hop if panel % 2 == 0 else len(order) - hop
        source = pick(order, lax.rem(here + len(order) - way, len(order)))
        owner, held = source // rows_held, lax.rem(source, rows_held)
        for at in range(slots):
            slot = owner * slots + at
            code = codes_ref[panel, slot]
            live = (code >= 0) & (code // NJ == held)
            found.append((live, slot, lax.rem(jnp.maximum(code, 0), NJ)))
    return found


def columns_of(found):
    hits = []
    for column in range(NJ):
        hit = jnp.bool_(False)
        for live, _, at in found:
            hit = hit | (live & (at == column))
        hits.append(hit)
    return hits


def fold_kernel(first, hops, later, order, rows_held, slots, band, codes_ref, ints_ref, *refs):
    chunks, rest = refs[: len(hops)], refs[len(hops) :]
    width = ints_ref.shape[2]
    found = chunk_updates(codes_ref, hops, order, rows_held, slots)
    if later is None:
        total_ref = rest[-1]
    elif later:
        total_ref, out_ref, sem = rest[-3], rest[-2], rest[-1]
        ready = [jnp.logical_not(hit) for hit in columns_of(chunk_updates(codes_ref, later, order, rows_held, slots))]
    else:
        total_ref, out_ref, sem = rest[0], rest[-2], rest[-1]
    def send(column):
        cols = pl.ds(pl.multiple_of(column * width, width), width)
        return pltpu.make_async_copy(
            total_ref.at[:, cols], out_ref.at[pl.ds(band[0], band[1]), cols], sem.at[column]
        )

    if first:
        total_ref[...] = jnp.zeros(total_ref.shape, jnp.float32)
    if later:
        hits = columns_of(found)
        for column in range(NJ):

            @pl.when(ready[column] & jnp.logical_not(hits[column]))
            def _():
                send(column).start()

    final = []
    for index, (live, slot, column) in enumerate(found):
        panel, chunk = hops[index // slots][0], chunks[index // slots]
        again = jnp.bool_(False)
        for other, _, at in found[index + 1 :]:
            again = again | (other & (at == column))
        final.append(live & jnp.logical_not(again))

        @pl.when(live)
        def _():
            cols = pl.ds(pl.multiple_of(column * width, width), width)
            total_ref[:, cols] += jnp.dot(
                chunk[...], ints_ref[panel, slot], preferred_element_type=jnp.float32
            )

        if later is not None and not later:

            @pl.when(final[-1])
            def _():
                send(column).start()

    if later:
        for column in range(NJ):

            @pl.when(ready[column] & hits[column])
            def _():
                send(column).start()

        for column in range(NJ):

            @pl.when(ready[column])
            def _():
                send(column).wait()

    elif later is not None:
        for done, (_, _, column) in zip(final, found):

            @pl.when(done)
            def _():
                send(column).wait()


def fold(codes, ints, chunks, hops, later, total, out, order, rows_held, slots, band, whole):
    first = total is None
    rows, width = chunks[0].shape
    vmem = pl.BlockSpec(memory_space=pltpu.VMEM)
    anywhere = pl.BlockSpec(memory_space=pl.ANY)
    operands = [codes, in_vmem(ints), *map(in_vmem, chunks)]
    in_specs = [pl.BlockSpec(memory_space=pltpu.SMEM)] + [vmem] * (1 + len(chunks))
    aliases, scratch, out_shapes, out_specs = {}, [], [], []
    if not first:
        operands.append(in_vmem(total))
        in_specs.append(vmem)
    if later is None or later:
        if not first:
            aliases[len(operands) - 1] = 0
        out_shapes.append(pltpu.VMEM((rows, NJ * width), jnp.float32))
        out_specs.append(vmem)
    if later is not None:
        if out is not None:
            aliases[len(operands)] = len(out_shapes)
            operands.append(out)
            in_specs.append(anywhere)
        out_shapes.append(jax.ShapeDtypeStruct(whole, jnp.float32))
        out_specs.append(anywhere)
        scratch = [pltpu.SemaphoreType.DMA((NJ,))]
    return pl.pallas_call(
        functools.partial(fold_kernel, first, hops, later, order, rows_held, slots, band),
        out_shape=out_shapes,
        in_specs=in_specs,
        out_specs=out_specs,
        scratch_shapes=scratch,
        input_output_aliases=aliases,
        compiler_params=pltpu.CompilerParams(vmem_limit_bytes=VMEM_LIMIT),
        cost_estimate=pl.CostEstimate(
            flops=2 * rows * width * width * len(hops) * slots,
            bytes_accessed=rows * NJ * width * 4,
            transcendentals=0,
        ),
        name="fold",
    )(*operands)


def body(amp_tiles, amp_rows, int_tiles, int_codes):
    n_row, n_col = lax.axis_size("row"), lax.axis_size("col")
    rows_held = n_row // n_col
    panels, slots, width = int_tiles.shape[0], int_tiles.shape[1], int_tiles.shape[3]
    across = n_col // CORES
    order = grid_cycle(n_row // across, across)
    forth = [(order[at], order[(at + 1) % n_row]) for at in range(n_row)]
    ways = [forth if panel % 2 == 0 else [(b, a) for a, b in forth] for panel in range(panels)]

    swap = [(c, c // CORES * CORES + (c + 1) % CORES) for c in range(n_col)]
    whole = (MI * width, NJ * width)
    cuts = [n_row - 2, n_row - 1, n_row]

    placed = place(amp_tiles, amp_rows, int_tiles, int_codes)
    streams, parcel = placed[:-1], placed[-1]
    parts, last = [], parcel
    for shift in range(1, n_col // CORES):
        moved = lax.optimization_barrier((parcel, last))[0] if shift > 1 else parcel
        moved = lax.ppermute(moved, "col", [(c, (c + shift * CORES) % n_col) for c in range(n_col)])
        last = lax.ppermute(moved, "col", swap)
        parts += [moved, last]
    last = lax.optimization_barrier((parcel, last))[0]
    parts = [parcel, lax.ppermute(last, "col", swap)] + parts

    codes, ints = collect(parts, panels, slots, rows_held * NJ + 1)
    rings = [[list(streams[group * panels : (group + 1) * panels])] for group in range(len(GROUPS))]
    totals, early, out = [None] * len(GROUPS), [None] * len(GROUPS), None
    for at in range(1, n_row):
        for group, (top, bottom) in enumerate(GROUPS):
            held = rings[group][-1]
            if at == n_row - 1:
                held = lax.optimization_barrier((early[group], held))[1]
            rings[group].append([lax.ppermute(held[panel], "row", ways[panel]) for panel in range(panels)])
        if at + 1 not in cuts:
            continue
        which = cuts.index(at + 1)
        begin = cuts[which - 1] if which else 0
        hops = [(panel, step) for step in range(begin, at + 1) for panel in range(panels)]
        later = None
        if which >= len(cuts) - 2:
            later = [(panel, step) for step in range(at + 1, n_row) for panel in range(panels)]
        for group, (top, bottom) in enumerate(GROUPS):
            chunks = [rings[group][step][panel] for panel, step in hops]
            band = (top * width, (bottom - top) * width)
            made = fold(
                codes, ints, chunks, hops, later, totals[group], out, order, rows_held, slots, band, whole
            )
            if later is None:
                totals[group] = early[group] = made[0]
            elif later:
                totals[group], out = made
            else:
                out = made[0]
    return out


def solution(mesh):
    return jax.shard_map(
        body,
        mesh=mesh,
        in_specs=(
            P(None, "col", "row", None, None),
            P(None, "col", "row"),
            P(None, "col", "row", None, None),
            P(None, "col", "row"),
        ),
        out_specs=P("col", "row"),
        check_vma=False,
    )
```

```python
import functools

import jax
import jax.numpy as jnp
from jax import lax
from jax.experimental import pallas as pl
from jax.experimental.pallas import tpu as pltpu
from jax.sharding import PartitionSpec as P

MI = 4
NJ = 6
CORES = 2
GROUPS = ((0, 2), (2, 4))
LINES = 16
VMEM_LIMIT = 8 * 1024 * 1024


def grid_cycle(depth, across):
    order = [z * across for z in range(depth)]
    for turn, z in enumerate(reversed(range(depth))):
        xs = range(1, across) if turn % 2 == 0 else range(across - 1, 0, -1)
        order += [z * across + x for x in xs]
    return order


def pick(table, index):
    value = jnp.int32(table[0])
    for at in range(1, len(table)):
        value = jnp.where(index == at, jnp.int32(table[at]), value)
    return value


def in_vmem(value):
    return pltpu.with_memory_space_constraint(value, pltpu.VMEM)


def in_hbm(value):
    return pltpu.with_memory_space_constraint(value, pltpu.HBM)


def place_kernel(rows_hbm, codes_hbm, tiles_hbm, ints_hbm, *rest):
    placed, parcel_ref = rest[: -1 - 6], rest[-1 - 6]
    rows_ref, codes_ref, tiles_ref, small_sem, tiles_sem, ints_sem = rest[-6:]
    panels, slots, width = tiles_ref.shape[0], tiles_ref.shape[1], tiles_ref.shape[2]
    held = ints_hbm.shape[1]
    small = [
        pltpu.make_async_copy(rows_hbm, rows_ref, small_sem.at[0]),
        pltpu.make_async_copy(codes_hbm, codes_ref, small_sem.at[1]),
    ]
    tiles = [
        pltpu.make_async_copy(tiles_hbm.at[panel, 0], tiles_ref.at[panel], tiles_sem.at[panel])
        for panel in range(panels)
    ]
    parcels = [
        pltpu.make_async_copy(
            ints_hbm.at[panel, at, 0],
            parcel_ref.at[pl.ds((panel * held + at) * width, width)],
            ints_sem.at[panel, at],
        )
        for panel in range(panels)
        for at in range(held)
    ]
    for copy in small + tiles + parcels:
        copy.start()
    for copy in small:
        copy.wait()
    lines = lax.broadcasted_iota(jnp.int32, (LINES, width), 0)
    labels = jnp.zeros((LINES, width), jnp.float32)
    for panel in range(panels):
        for at in range(held):
            code = codes_ref[panel, 0, at].astype(jnp.float32)
            labels = jnp.where(lines == panel * held + at, code, labels)
    parcel_ref[pl.ds(panels * held * width, LINES)] = labels.astype(parcel_ref.dtype)
    for panel in range(panels):
        tiles[panel].wait()
        for group, (first, last) in enumerate(GROUPS):
            for row in range(first, last):
                slot = jnp.int32(-1)
                for at in range(slots):
                    slot = jnp.where(rows_ref[panel, 0, at] == row, at, slot)
                spot = placed[group * panels + panel].at[pl.ds((row - first) * width, width)]

                @pl.when(slot >= 0)
                def _():
                    spot[...] = tiles_ref[panel, jnp.maximum(slot, 0)]

                @pl.when(slot < 0)
                def _():
                    spot[...] = jnp.zeros(spot.shape, spot.dtype)

    for copy in parcels:
        copy.wait()


def place(amp_tiles, amp_rows, int_tiles, int_codes):
    panels, held, slots, width = amp_tiles.shape[0], int_tiles.shape[1], amp_tiles.shape[2], amp_tiles.shape[3]
    codes = jnp.transpose(int_codes, (0, 2, 1))
    shapes = [
        pltpu.VMEM(((last - first) * width, width), amp_tiles.dtype)
        for first, last in GROUPS
        for _ in range(panels)
    ]
    shapes.append(pltpu.VMEM((panels * held * width + LINES, width), int_tiles.dtype))
    return pl.pallas_call(
        place_kernel,
        out_shape=shapes,
        in_specs=[pl.BlockSpec(memory_space=pl.ANY)] * 4,
        out_specs=[pl.BlockSpec(memory_space=pltpu.VMEM)] * len(shapes),
        scratch_shapes=[
            pltpu.SMEM(amp_rows.shape, jnp.int32),
            pltpu.SMEM(codes.shape, jnp.int32),
            pltpu.VMEM((panels, slots, width, width), amp_tiles.dtype),
            pltpu.SemaphoreType.DMA((2,)),
            pltpu.SemaphoreType.DMA((panels,)),
            pltpu.SemaphoreType.DMA((panels, held)),
        ],
        compiler_params=pltpu.CompilerParams(vmem_limit_bytes=VMEM_LIMIT),
        name="place",
    )(in_hbm(amp_rows), in_hbm(codes), in_hbm(amp_tiles), in_hbm(int_tiles))


def join_kernel(*refs):
    size = refs[0].shape[0]
    for at, ref in enumerate(refs[:-1]):
        refs[-1][pl.ds(at * size, size)] = ref[...]


def join(parts):
    size, width = parts[0].shape
    vmem = pl.BlockSpec(memory_space=pltpu.VMEM)
    return pl.pallas_call(
        join_kernel,
        out_shape=pltpu.VMEM((size * len(parts), width), parts[0].dtype),
        in_specs=[vmem] * len(parts),
        out_specs=vmem,
        compiler_params=pltpu.CompilerParams(vmem_limit_bytes=VMEM_LIMIT),
        name="join",
    )(*map(in_vmem, parts))


def collect_kernel(panels, slots, base, *refs):
    refs, totals = refs[: -len(GROUPS)], refs[-len(GROUPS) :]
    joined, codes_ref, out_ref = refs[:-2], refs[-2], refs[-1]
    width = joined[0].shape[1]
    size = panels * slots * width + LINES
    depth = len(joined)
    parts = [joined[shift].at[pl.ds(flip * size, size)] for shift in range(depth) for flip in range(CORES)]
    col = lax.axis_index("col")
    y, core = col // CORES, lax.rem(col, CORES)
    owners = []
    for at, part in enumerate(parts):
        shift, flip = at // CORES, at % CORES
        owner = lax.rem(y + depth - shift, depth) * CORES + lax.rem(core + flip, CORES)
        owners.append(owner)
        for panel in range(panels):
            for slot in range(slots):
                out_ref[panel, owner * slots + slot] = part[pl.ds((panel * slots + slot) * width, width)]
    lines = lax.broadcasted_iota(jnp.int32, (LINES, width), 0)
    scale = jnp.zeros((LINES, width), jnp.float32)
    for at in range(panels * slots):
        scale = jnp.where(lines == at, float(base**at), scale)
    for owner, part in zip(owners, parts):
        labels = part[pl.ds(panels * slots * width, LINES), pl.ds(0, 128)].astype(jnp.float32) + 1.0
        number = jnp.sum(labels * scale[:, :128], axis=0, keepdims=True)
        digits = jnp.max(number).astype(jnp.int32)
        for panel in range(panels):
            for slot in range(slots):
                codes_ref[panel, owner * slots + slot] = lax.rem(digits, base) - 1
                digits = digits // base
    for total_ref in totals:
        total_ref[...] = jnp.zeros(total_ref.shape, jnp.float32)


def collect(parts, panels, slots, base):
    width = parts[0].shape[1]
    total = slots * CORES * len(parts)
    assert base ** (panels * slots) < 2**24
    vmem = pl.BlockSpec(memory_space=pltpu.VMEM)
    return pl.pallas_call(
        functools.partial(collect_kernel, panels, slots, base),
        out_shape=[
            pltpu.SMEM((panels, total), jnp.int32),
            pltpu.VMEM((panels, total, width, width), parts[0].dtype),
            *(pltpu.VMEM(((last - first) * width, NJ * width), jnp.float32) for first, last in GROUPS),
        ],
        in_specs=[vmem] * len(parts),
        out_specs=[pl.BlockSpec(memory_space=pltpu.SMEM)] + [vmem] * (1 + len(GROUPS)),
        compiler_params=pltpu.CompilerParams(vmem_limit_bytes=VMEM_LIMIT),
        name="collect",
    )(*map(in_vmem, parts))


def chunk_updates(codes_ref, hops, order, rows_held, slots):
    me = lax.axis_index("row")
    inverse = [order.index(at) for at in range(len(order))]
    here = pick(inverse, me)
    found = []
    for panel, hop in hops:
        way = hop if panel % 2 == 0 else len(order) - hop
        source = pick(order, lax.rem(here + len(order) - way, len(order)))
        owner, held = source // rows_held, lax.rem(source, rows_held)
        for at in range(slots):
            slot = owner * slots + at
            code = codes_ref[panel, slot]
            live = (code >= 0) & (code // NJ == held)
            found.append((live, slot, lax.rem(jnp.maximum(code, 0), NJ)))
    return found


def columns_of(found):
    hits = []
    for column in range(NJ):
        hit = jnp.bool_(False)
        for live, _, at in found:
            hit = hit | (live & (at == column))
        hits.append(hit)
    return hits


def fold_kernel(first, hops, later, order, rows_held, slots, band, codes_ref, ints_ref, *refs):
    chunks, rest = refs[: len(hops)], refs[len(hops) :]
    width = ints_ref.shape[2]
    found = chunk_updates(codes_ref, hops, order, rows_held, slots)
    if later is None:
        total_ref = rest[-1]
    elif later:
        total_ref, out_ref, sem = rest[-3], rest[-2], rest[-1]
        ready = [jnp.logical_not(hit) for hit in columns_of(chunk_updates(codes_ref, later, order, rows_held, slots))]
    else:
        total_ref, out_ref, sem = rest[0], rest[-2], rest[-1]
    def send(column):
        cols = pl.ds(pl.multiple_of(column * width, width), width)
        return pltpu.make_async_copy(
            total_ref.at[:, cols], out_ref.at[pl.ds(band[0], band[1]), cols], sem.at[column]
        )

    if first:
        total_ref[...] = jnp.zeros(total_ref.shape, jnp.float32)
    if later:
        hits = columns_of(found)
        for column in range(NJ):

            @pl.when(ready[column] & jnp.logical_not(hits[column]))
            def _():
                send(column).start()

    final = []
    for index, (live, slot, column) in enumerate(found):
        panel, chunk = hops[index // slots][0], chunks[index // slots]
        again = jnp.bool_(False)
        for other, _, at in found[index + 1 :]:
            again = again | (other & (at == column))
        final.append(live & jnp.logical_not(again))

        @pl.when(live)
        def _():
            cols = pl.ds(pl.multiple_of(column * width, width), width)
            total_ref[:, cols] += jnp.dot(
                chunk[...], ints_ref[panel, slot], preferred_element_type=jnp.float32
            )

        if later is not None and not later:

            @pl.when(final[-1])
            def _():
                send(column).start()

    if later:
        for column in range(NJ):

            @pl.when(ready[column] & hits[column])
            def _():
                send(column).start()

        for column in range(NJ):

            @pl.when(ready[column])
            def _():
                send(column).wait()

    elif later is not None:
        for done, (_, _, column) in zip(final, found):

            @pl.when(done)
            def _():
                send(column).wait()


def fold(codes, ints, chunks, hops, later, total, out, order, rows_held, slots, band, whole):
    first = total is None
    rows, width = chunks[0].shape
    vmem = pl.BlockSpec(memory_space=pltpu.VMEM)
    anywhere = pl.BlockSpec(memory_space=pl.ANY)
    operands = [pltpu.with_memory_space_constraint(codes, pltpu.SMEM), in_vmem(ints), *map(in_vmem, chunks)]
    in_specs = [pl.BlockSpec(memory_space=pltpu.SMEM)] + [vmem] * (1 + len(chunks))
    aliases, scratch, out_shapes, out_specs = {}, [], [], []
    if not first:
        operands.append(in_vmem(total))
        in_specs.append(vmem)
    if later is None or later:
        if not first:
            aliases[len(operands) - 1] = 0
        out_shapes.append(pltpu.VMEM((rows, NJ * width), jnp.float32))
        out_specs.append(vmem)
    if later is not None:
        if out is not None:
            aliases[len(operands)] = len(out_shapes)
            operands.append(out)
            in_specs.append(anywhere)
        out_shapes.append(jax.ShapeDtypeStruct(whole, jnp.float32))
        out_specs.append(anywhere)
        scratch = [pltpu.SemaphoreType.DMA((NJ,))]
    return pl.pallas_call(
        functools.partial(fold_kernel, first, hops, later, order, rows_held, slots, band),
        out_shape=out_shapes,
        in_specs=in_specs,
        out_specs=out_specs,
        scratch_shapes=scratch,
        input_output_aliases=aliases,
        compiler_params=pltpu.CompilerParams(vmem_limit_bytes=VMEM_LIMIT),
        cost_estimate=pl.CostEstimate(
            flops=2 * rows * width * width * len(hops) * slots,
            bytes_accessed=rows * NJ * width * 4,
            transcendentals=0,
        ),
        name="fold",
    )(*operands)


def body(amp_tiles, amp_rows, int_tiles, int_codes):
    n_row, n_col = lax.axis_size("row"), lax.axis_size("col")
    rows_held = n_row // n_col
    panels, slots, width = int_tiles.shape[0], int_tiles.shape[1], int_tiles.shape[3]
    across = n_col // CORES
    order = grid_cycle(n_row // across, across)
    forth = [(order[at], order[(at + 1) % n_row]) for at in range(n_row)]
    ways = [forth if panel % 2 == 0 else [(b, a) for a, b in forth] for panel in range(panels)]

    swap = [(c, c // CORES * CORES + (c + 1) % CORES) for c in range(n_col)]
    whole = (MI * width, NJ * width)
    cuts = [n_row - 3, n_row - 1, n_row]

    placed = place(amp_tiles, amp_rows, int_tiles, int_codes)
    streams, parcel = placed[:-1], placed[-1]
    parts = [join([parcel, lax.ppermute(parcel, "col", swap)])]
    for shift in range(1, n_col // CORES):
        moved = lax.optimization_barrier((parts[0], parts[-1]))[0] if shift > 1 else parts[0]
        parts.append(lax.ppermute(moved, "col", [(c, (c + shift * CORES) % n_col) for c in range(n_col)]))
    codes, ints, *totals = collect(parts, panels, slots, rows_held * NJ + 1)
    rings = [[list(streams[group * panels : (group + 1) * panels])] for group in range(len(GROUPS))]
    early, out = [None] * len(GROUPS), None
    for at in range(1, n_row):
        for group, (top, bottom) in enumerate(GROUPS):
            held = rings[group][-1]
            if at == n_row - 2 and group == len(GROUPS) - 1:
                held = [lax.optimization_barrier((ints, one))[1] for one in held]
            if at == n_row - 1:
                held = [lax.optimization_barrier((early[group], one))[1] for one in held]
            rings[group].append([lax.ppermute(held[panel], "row", ways[panel]) for panel in range(panels)])
        if at + 1 not in cuts:
            continue
        which = cuts.index(at + 1)
        begin = cuts[which - 1] if which else 0
        hops = [(panel, step) for step in range(begin, at + 1) for panel in range(panels)]
        later = None
        if which >= len(cuts) - 2:
            later = [(panel, step) for step in range(at + 1, n_row) for panel in range(panels)]
        for group, (top, bottom) in enumerate(GROUPS):
            chunks = [rings[group][step][panel] for panel, step in hops]
            band = (top * width, (bottom - top) * width)
            made = fold(
                codes, ints, chunks, hops, later, totals[group], out, order, rows_held, slots, band, whole
            )
            if later is None:
                totals[group] = early[group] = made[0]
            elif later:
                totals[group], out = made
            else:
                out = made[0]
    return out


def solution(mesh):
    return jax.shard_map(
        body,
        mesh=mesh,
        in_specs=(
            P(None, "col", "row", None, None),
            P(None, "col", "row"),
            P(None, "col", "row", None, None),
            P(None, "col", "row"),
        ),
        out_specs=P("col", "row"),
        check_vma=False,
    )
```

```python
import functools

import jax
import jax.numpy as jnp
from jax import lax
from jax.experimental import pallas as pl
from jax.experimental.pallas import tpu as pltpu
from jax.sharding import PartitionSpec as P

MI = 4
NJ = 6
CORES = 2
GROUPS = ((0, 2), (2, 4))
LINES = 16
VMEM_LIMIT = 8 * 1024 * 1024


def grid_cycle(depth, across):
    order = [z * across for z in range(depth)]
    for turn, z in enumerate(reversed(range(depth))):
        xs = range(1, across) if turn % 2 == 0 else range(across - 1, 0, -1)
        order += [z * across + x for x in xs]
    return order


def pick(table, index):
    value = jnp.int32(table[0])
    for at in range(1, len(table)):
        value = jnp.where(index == at, jnp.int32(table[at]), value)
    return value


def in_vmem(value):
    return pltpu.with_memory_space_constraint(value, pltpu.VMEM)


def in_hbm(value):
    return pltpu.with_memory_space_constraint(value, pltpu.HBM)


def place_kernel(rows_hbm, codes_hbm, tiles_hbm, ints_hbm, *rest):
    placed, parcel_ref = rest[: -1 - 6], rest[-1 - 6]
    rows_ref, codes_ref, tiles_ref, small_sem, tiles_sem, ints_sem = rest[-6:]
    panels, slots, width = tiles_ref.shape[0], tiles_ref.shape[1], tiles_ref.shape[2]
    held = ints_hbm.shape[1]
    small = [
        pltpu.make_async_copy(rows_hbm, rows_ref, small_sem.at[0]),
        pltpu.make_async_copy(codes_hbm, codes_ref, small_sem.at[1]),
    ]
    tiles = [
        pltpu.make_async_copy(tiles_hbm.at[panel, 0], tiles_ref.at[panel], tiles_sem.at[panel])
        for panel in range(panels)
    ]
    parcels = [
        pltpu.make_async_copy(
            ints_hbm.at[panel, at, 0],
            parcel_ref.at[pl.ds((panel * held + at) * width, width)],
            ints_sem.at[panel, at],
        )
        for panel in range(panels)
        for at in range(held)
    ]
    for copy in small + tiles + parcels:
        copy.start()
    for copy in small:
        copy.wait()
    lines = lax.broadcasted_iota(jnp.int32, (LINES, width), 0)
    labels = jnp.zeros((LINES, width), jnp.float32)
    for panel in range(panels):
        for at in range(held):
            code = codes_ref[panel, 0, at].astype(jnp.float32)
            labels = jnp.where(lines == panel * held + at, code, labels)
    parcel_ref[pl.ds(panels * held * width, LINES)] = labels.astype(parcel_ref.dtype)
    for panel in range(panels):
        tiles[panel].wait()
        for group, (first, last) in enumerate(GROUPS):
            for row in range(first, last):
                slot = jnp.int32(-1)
                for at in range(slots):
                    slot = jnp.where(rows_ref[panel, 0, at] == row, at, slot)
                spot = placed[group * panels + panel].at[pl.ds((row - first) * width, width)]

                @pl.when(slot >= 0)
                def _():
                    spot[...] = tiles_ref[panel, jnp.maximum(slot, 0)]

                @pl.when(slot < 0)
                def _():
                    spot[...] = jnp.zeros(spot.shape, spot.dtype)

    for copy in parcels:
        copy.wait()


def place(amp_tiles, amp_rows, int_tiles, int_codes):
    panels, held, slots, width = amp_tiles.shape[0], int_tiles.shape[1], amp_tiles.shape[2], amp_tiles.shape[3]
    codes = jnp.transpose(int_codes, (0, 2, 1))
    shapes = [
        pltpu.VMEM(((last - first) * width, width), amp_tiles.dtype)
        for first, last in GROUPS
        for _ in range(panels)
    ]
    shapes.append(pltpu.VMEM((panels * held * width + LINES, width), int_tiles.dtype))
    return pl.pallas_call(
        place_kernel,
        out_shape=shapes,
        in_specs=[pl.BlockSpec(memory_space=pl.ANY)] * 4,
        out_specs=[pl.BlockSpec(memory_space=pltpu.VMEM)] * len(shapes),
        scratch_shapes=[
            pltpu.SMEM(amp_rows.shape, jnp.int32),
            pltpu.SMEM(codes.shape, jnp.int32),
            pltpu.VMEM((panels, slots, width, width), amp_tiles.dtype),
            pltpu.SemaphoreType.DMA((2,)),
            pltpu.SemaphoreType.DMA((panels,)),
            pltpu.SemaphoreType.DMA((panels, held)),
        ],
        compiler_params=pltpu.CompilerParams(vmem_limit_bytes=VMEM_LIMIT),
        name="place",
    )(in_hbm(amp_rows), in_hbm(codes), in_hbm(amp_tiles), in_hbm(int_tiles))


def join_kernel(*refs):
    size = refs[0].shape[0]
    for at, ref in enumerate(refs[:-1]):
        refs[-1][pl.ds(at * size, size)] = ref[...]


def join(parts):
    size, width = parts[0].shape
    vmem = pl.BlockSpec(memory_space=pltpu.VMEM)
    return pl.pallas_call(
        join_kernel,
        out_shape=pltpu.VMEM((size * len(parts), width), parts[0].dtype),
        in_specs=[vmem] * len(parts),
        out_specs=vmem,
        compiler_params=pltpu.CompilerParams(vmem_limit_bytes=VMEM_LIMIT),
        name="join",
    )(*map(in_vmem, parts))


def collect_kernel(panels, slots, base, *refs):
    refs, totals = refs[: -len(GROUPS)], refs[-len(GROUPS) :]
    joined, codes_ref, out_ref = refs[:-2], refs[-2], refs[-1]
    width = joined[0].shape[1]
    size = panels * slots * width + LINES
    depth = len(joined)
    parts = [joined[shift].at[pl.ds(flip * size, size)] for shift in range(depth) for flip in range(CORES)]
    col = lax.axis_index("col")
    y, core = col // CORES, lax.rem(col, CORES)
    owners = []
    for at, part in enumerate(parts):
        shift, flip = at // CORES, at % CORES
        owner = lax.rem(y + depth - shift, depth) * CORES + lax.rem(core + flip, CORES)
        owners.append(owner)
        for panel in range(panels):
            for slot in range(slots):
                out_ref[panel, owner * slots + slot] = part[pl.ds((panel * slots + slot) * width, width)]
    lines = lax.broadcasted_iota(jnp.int32, (LINES, width), 0)
    scale = jnp.zeros((LINES, width), jnp.float32)
    for at in range(panels * slots):
        scale = jnp.where(lines == at, float(base**at), scale)
    for owner, part in zip(owners, parts):
        labels = part[pl.ds(panels * slots * width, LINES), pl.ds(0, 128)].astype(jnp.float32) + 1.0
        number = jnp.sum(labels * scale[:, :128], axis=0, keepdims=True)
        digits = jnp.max(number).astype(jnp.int32)
        for panel in range(panels):
            for slot in range(slots):
                codes_ref[panel, owner * slots + slot] = lax.rem(digits, base) - 1
                digits = digits // base
    for total_ref in totals:
        total_ref[...] = jnp.zeros(total_ref.shape, jnp.float32)


def collect(parts, panels, slots, base):
    width = parts[0].shape[1]
    total = slots * CORES * len(parts)
    assert base ** (panels * slots) < 2**24
    vmem = pl.BlockSpec(memory_space=pltpu.VMEM)
    return pl.pallas_call(
        functools.partial(collect_kernel, panels, slots, base),
        out_shape=[
            pltpu.SMEM((panels, total), jnp.int32),
            pltpu.VMEM((panels, total, width, width), parts[0].dtype),
            *(pltpu.VMEM(((last - first) * width, NJ * width), jnp.float32) for first, last in GROUPS),
        ],
        in_specs=[vmem] * len(parts),
        out_specs=[pl.BlockSpec(memory_space=pltpu.SMEM)] + [vmem] * (1 + len(GROUPS)),
        compiler_params=pltpu.CompilerParams(vmem_limit_bytes=VMEM_LIMIT),
        name="collect",
    )(*map(in_vmem, parts))


def chunk_updates(codes_ref, hops, order, rows_held, slots):
    me = lax.axis_index("row")
    inverse = [order.index(at) for at in range(len(order))]
    here = pick(inverse, me)
    found = []
    for panel, hop in hops:
        way = hop if panel % 2 == 0 else len(order) - hop
        source = pick(order, lax.rem(here + len(order) - way, len(order)))
        owner, held = source // rows_held, lax.rem(source, rows_held)
        for at in range(slots):
            slot = owner * slots + at
            code = codes_ref[panel, slot]
            live = (code >= 0) & (code // NJ == held)
            found.append((live, slot, lax.rem(jnp.maximum(code, 0), NJ)))
    return found


def columns_of(found):
    hits = []
    for column in range(NJ):
        hit = jnp.bool_(False)
        for live, _, at in found:
            hit = hit | (live & (at == column))
        hits.append(hit)
    return hits


def fold_kernel(first, hops, later, order, rows_held, slots, band, codes_ref, ints_ref, *refs):
    chunks, rest = refs[: len(hops)], refs[len(hops) :]
    width = ints_ref.shape[2]
    found = chunk_updates(codes_ref, hops, order, rows_held, slots)
    if later is None:
        total_ref = rest[-1]
    elif later:
        total_ref, out_ref, sem = rest[-3], rest[-2], rest[-1]
        ready = [jnp.logical_not(hit) for hit in columns_of(chunk_updates(codes_ref, later, order, rows_held, slots))]
    else:
        total_ref, out_ref, sem = rest[0], rest[-2], rest[-1]
    def send(column):
        cols = pl.ds(pl.multiple_of(column * width, width), width)
        return pltpu.make_async_copy(
            total_ref.at[:, cols], out_ref.at[pl.ds(band[0], band[1]), cols], sem.at[column]
        )

    if first:
        total_ref[...] = jnp.zeros(total_ref.shape, jnp.float32)
    if later:
        hits = columns_of(found)
        for column in range(NJ):

            @pl.when(ready[column] & jnp.logical_not(hits[column]))
            def _():
                send(column).start()

    final = []
    for index, (live, slot, column) in enumerate(found):
        panel, chunk = hops[index // slots][0], chunks[index // slots]
        again = jnp.bool_(False)
        for other, _, at in found[index + 1 :]:
            again = again | (other & (at == column))
        final.append(live & jnp.logical_not(again))

        @pl.when(live)
        def _():
            cols = pl.ds(pl.multiple_of(column * width, width), width)
            total_ref[:, cols] += jnp.dot(
                chunk[...], ints_ref[panel, slot], preferred_element_type=jnp.float32
            )

        if later is not None and not later:

            @pl.when(final[-1])
            def _():
                send(column).start()

    if later:
        for column in range(NJ):

            @pl.when(ready[column] & hits[column])
            def _():
                send(column).start()

        for column in range(NJ):

            @pl.when(ready[column])
            def _():
                send(column).wait()

    elif later is not None:
        for done, (_, _, column) in zip(final, found):

            @pl.when(done)
            def _():
                send(column).wait()


def fold(codes, ints, chunks, hops, later, total, out, order, rows_held, slots, band, whole):
    first = total is None
    rows, width = chunks[0].shape
    vmem = pl.BlockSpec(memory_space=pltpu.VMEM)
    anywhere = pl.BlockSpec(memory_space=pl.ANY)
    operands = [pltpu.with_memory_space_constraint(codes, pltpu.SMEM), in_vmem(ints), *map(in_vmem, chunks)]
    in_specs = [pl.BlockSpec(memory_space=pltpu.SMEM)] + [vmem] * (1 + len(chunks))
    aliases, scratch, out_shapes, out_specs = {}, [], [], []
    if not first:
        operands.append(in_vmem(total))
        in_specs.append(vmem)
    if later is None or later:
        if not first:
            aliases[len(operands) - 1] = 0
        out_shapes.append(pltpu.VMEM((rows, NJ * width), jnp.float32))
        out_specs.append(vmem)
    if later is not None:
        if out is not None:
            aliases[len(operands)] = len(out_shapes)
            operands.append(out)
            in_specs.append(anywhere)
        out_shapes.append(jax.ShapeDtypeStruct(whole, jnp.float32))
        out_specs.append(anywhere)
        scratch = [pltpu.SemaphoreType.DMA((NJ,))]
    return pl.pallas_call(
        functools.partial(fold_kernel, first, hops, later, order, rows_held, slots, band),
        out_shape=out_shapes,
        in_specs=in_specs,
        out_specs=out_specs,
        scratch_shapes=scratch,
        input_output_aliases=aliases,
        compiler_params=pltpu.CompilerParams(vmem_limit_bytes=VMEM_LIMIT),
        cost_estimate=pl.CostEstimate(
            flops=2 * rows * width * width * len(hops) * slots,
            bytes_accessed=rows * NJ * width * 4,
            transcendentals=0,
        ),
        name="fold",
    )(*operands)


def body(amp_tiles, amp_rows, int_tiles, int_codes):
    n_row, n_col = lax.axis_size("row"), lax.axis_size("col")
    rows_held = n_row // n_col
    panels, slots, width = int_tiles.shape[0], int_tiles.shape[1], int_tiles.shape[3]
    across = n_col // CORES
    order = grid_cycle(n_row // across, across)[::-1]
    forth = [(order[at], order[(at + 1) % n_row]) for at in range(n_row)]
    ways = [forth if panel % 2 == 0 else [(b, a) for a, b in forth] for panel in range(panels)]

    swap = [(c, c // CORES * CORES + (c + 1) % CORES) for c in range(n_col)]
    whole = (MI * width, NJ * width)
    cuts = [n_row - 3, n_row - 1, n_row]

    placed = place(amp_tiles, amp_rows, int_tiles, int_codes)
    streams, parcel = placed[:-1], placed[-1]
    parts = [join([parcel, lax.ppermute(parcel, "col", swap)])]
    for shift in range(1, n_col // CORES):
        moved = lax.optimization_barrier((parts[0], parts[-1]))[0] if shift > 1 else parts[0]
        parts.append(lax.ppermute(moved, "col", [(c, (c + shift * CORES) % n_col) for c in range(n_col)]))
    codes, ints, *totals = collect(parts, panels, slots, rows_held * NJ + 1)
    rings = [[list(streams[group * panels : (group + 1) * panels])] for group in range(len(GROUPS))]
    early, out = [None] * len(GROUPS), None
    for at in range(1, n_row):
        for group, (top, bottom) in enumerate(GROUPS):
            held = rings[group][-1]
            if at == n_row - 2 and group == len(GROUPS) - 1:
                held = [lax.optimization_barrier((ints, one))[1] for one in held]
            if at == n_row - 1:
                held = [lax.optimization_barrier((early[group], one))[1] for one in held]
            rings[group].append([lax.ppermute(held[panel], "row", ways[panel]) for panel in range(panels)])
        if at + 1 not in cuts:
            continue
        which = cuts.index(at + 1)
        begin = cuts[which - 1] if which else 0
        hops = [(panel, step) for step in range(begin, at + 1) for panel in range(panels)]
        later = None
        if which >= len(cuts) - 2:
            later = [(panel, step) for step in range(at + 1, n_row) for panel in range(panels)]
        for group, (top, bottom) in enumerate(GROUPS):
            chunks = [rings[group][step][panel] for panel, step in hops]
            band = (top * width, (bottom - top) * width)
            made = fold(
                codes, ints, chunks, hops, later, totals[group], out, order, rows_held, slots, band, whole
            )
            if later is None:
                totals[group] = early[group] = made[0]
            elif later:
                totals[group], out = made
            else:
                out = made[0]
    return out


def solution(mesh):
    return jax.shard_map(
        body,
        mesh=mesh,
        in_specs=(
            P(None, "col", "row", None, None),
            P(None, "col", "row"),
            P(None, "col", "row", None, None),
            P(None, "col", "row"),
        ),
        out_specs=P("col", "row"),
        check_vma=False,
    )
```

```python
import functools

import jax
import jax.numpy as jnp
from jax import lax
from jax.experimental import pallas as pl
from jax.experimental.pallas import tpu as pltpu
from jax.sharding import PartitionSpec as P

MI = 4
NJ = 6
CORES = 2
GROUPS = ((0, MI),)
LINES = 16
VMEM_LIMIT = 8 * 1024 * 1024


def grid_cycle(depth, across):
    order = [z * across for z in range(depth)]
    for turn, z in enumerate(reversed(range(depth))):
        xs = range(1, across) if turn % 2 == 0 else range(across - 1, 0, -1)
        order += [z * across + x for x in xs]
    return order


def pick(table, index):
    value = jnp.int32(table[0])
    for at in range(1, len(table)):
        value = jnp.where(index == at, jnp.int32(table[at]), value)
    return value


def in_vmem(value):
    return pltpu.with_memory_space_constraint(value, pltpu.VMEM)


def in_hbm(value):
    return pltpu.with_memory_space_constraint(value, pltpu.HBM)


def place_kernel(rows_hbm, codes_hbm, tiles_hbm, ints_hbm, *rest):
    placed, parcel_ref = rest[: -1 - 6], rest[-1 - 6]
    rows_ref, codes_ref, tiles_ref, small_sem, tiles_sem, ints_sem = rest[-6:]
    panels, slots, width = tiles_ref.shape[0], tiles_ref.shape[1], tiles_ref.shape[2]
    held = ints_hbm.shape[1]
    small = [
        pltpu.make_async_copy(rows_hbm, rows_ref, small_sem.at[0]),
        pltpu.make_async_copy(codes_hbm, codes_ref, small_sem.at[1]),
    ]
    tiles = [
        pltpu.make_async_copy(tiles_hbm.at[panel, 0], tiles_ref.at[panel], tiles_sem.at[panel])
        for panel in range(panels)
    ]
    parcels = [
        pltpu.make_async_copy(
            ints_hbm.at[panel, at, 0],
            parcel_ref.at[pl.ds((panel * held + at) * width, width)],
            ints_sem.at[panel, at],
        )
        for panel in range(panels)
        for at in range(held)
    ]
    for copy in small + tiles + parcels:
        copy.start()
    for copy in small:
        copy.wait()
    lines = lax.broadcasted_iota(jnp.int32, (LINES, width), 0)
    labels = jnp.zeros((LINES, width), jnp.float32)
    for panel in range(panels):
        for at in range(held):
            code = codes_ref[panel, 0, at].astype(jnp.float32)
            labels = jnp.where(lines == panel * held + at, code, labels)
    parcel_ref[pl.ds(panels * held * width, LINES)] = labels.astype(parcel_ref.dtype)
    for panel in range(panels):
        tiles[panel].wait()
        for group, (first, last) in enumerate(GROUPS):
            for row in range(first, last):
                slot = jnp.int32(-1)
                for at in range(slots):
                    slot = jnp.where(rows_ref[panel, 0, at] == row, at, slot)
                spot = placed[group * panels + panel].at[pl.ds((row - first) * width, width)]

                @pl.when(slot >= 0)
                def _():
                    spot[...] = tiles_ref[panel, jnp.maximum(slot, 0)]

                @pl.when(slot < 0)
                def _():
                    spot[...] = jnp.zeros(spot.shape, spot.dtype)

    for copy in parcels:
        copy.wait()


def place(amp_tiles, amp_rows, int_tiles, int_codes):
    panels, held, slots, width = amp_tiles.shape[0], int_tiles.shape[1], amp_tiles.shape[2], amp_tiles.shape[3]
    codes = jnp.transpose(int_codes, (0, 2, 1))
    shapes = [
        pltpu.VMEM(((last - first) * width, width), amp_tiles.dtype)
        for first, last in GROUPS
        for _ in range(panels)
    ]
    shapes.append(pltpu.VMEM((panels * held * width + LINES, width), int_tiles.dtype))
    return pl.pallas_call(
        place_kernel,
        out_shape=shapes,
        in_specs=[pl.BlockSpec(memory_space=pl.ANY)] * 4,
        out_specs=[pl.BlockSpec(memory_space=pltpu.VMEM)] * len(shapes),
        scratch_shapes=[
            pltpu.SMEM(amp_rows.shape, jnp.int32),
            pltpu.SMEM(codes.shape, jnp.int32),
            pltpu.VMEM((panels, slots, width, width), amp_tiles.dtype),
            pltpu.SemaphoreType.DMA((2,)),
            pltpu.SemaphoreType.DMA((panels,)),
            pltpu.SemaphoreType.DMA((panels, held)),
        ],
        compiler_params=pltpu.CompilerParams(vmem_limit_bytes=VMEM_LIMIT),
        name="place",
    )(in_hbm(amp_rows), in_hbm(codes), in_hbm(amp_tiles), in_hbm(int_tiles))


def split_kernel(*refs):
    count = len(refs) // 3
    for at, ref in enumerate(refs[:count]):
        size = ref.shape[0] // 2
        for half in range(2):
            refs[count + half * count + at][...] = ref[pl.ds(half * size, size)]


def split(chunks):
    rows, width = chunks[0].shape
    vmem = pl.BlockSpec(memory_space=pltpu.VMEM)
    made = pl.pallas_call(
        split_kernel,
        out_shape=[pltpu.VMEM((rows // 2, width), chunks[0].dtype)] * (2 * len(chunks)),
        in_specs=[vmem] * len(chunks),
        out_specs=[vmem] * (2 * len(chunks)),
        compiler_params=pltpu.CompilerParams(vmem_limit_bytes=VMEM_LIMIT),
        name="split",
    )(*map(in_vmem, chunks))
    return made[: len(chunks)], made[len(chunks) :]


def join_kernel(*refs):
    size = refs[0].shape[0]
    for at, ref in enumerate(refs[:-1]):
        refs[-1][pl.ds(at * size, size)] = ref[...]


def join(parts):
    size, width = parts[0].shape
    vmem = pl.BlockSpec(memory_space=pltpu.VMEM)
    return pl.pallas_call(
        join_kernel,
        out_shape=pltpu.VMEM((size * len(parts), width), parts[0].dtype),
        in_specs=[vmem] * len(parts),
        out_specs=vmem,
        compiler_params=pltpu.CompilerParams(vmem_limit_bytes=VMEM_LIMIT),
        name="join",
    )(*map(in_vmem, parts))


def collect_kernel(panels, slots, base, *refs):
    refs, totals = refs[: -len(GROUPS)], refs[-len(GROUPS) :]
    joined, codes_ref, out_ref = refs[:-2], refs[-2], refs[-1]
    width = joined[0].shape[1]
    size = panels * slots * width + LINES
    depth = len(joined)
    parts = [joined[shift].at[pl.ds(flip * size, size)] for shift in range(depth) for flip in range(CORES)]
    col = lax.axis_index("col")
    y, core = col // CORES, lax.rem(col, CORES)
    owners = []
    for at, part in enumerate(parts):
        shift, flip = at // CORES, at % CORES
        owner = lax.rem(y + depth - shift, depth) * CORES + lax.rem(core + flip, CORES)
        owners.append(owner)
        for panel in range(panels):
            for slot in range(slots):
                out_ref[panel, owner * slots + slot] = part[pl.ds((panel * slots + slot) * width, width)]
    lines = lax.broadcasted_iota(jnp.int32, (LINES, width), 0)
    scale = jnp.zeros((LINES, width), jnp.float32)
    for at in range(panels * slots):
        scale = jnp.where(lines == at, float(base**at), scale)
    for owner, part in zip(owners, parts):
        labels = part[pl.ds(panels * slots * width, LINES), pl.ds(0, 128)].astype(jnp.float32) + 1.0
        number = jnp.sum(labels * scale[:, :128], axis=0, keepdims=True)
        digits = jnp.max(number).astype(jnp.int32)
        for panel in range(panels):
            for slot in range(slots):
                codes_ref[panel, owner * slots + slot] = lax.rem(digits, base) - 1
                digits = digits // base
    for total_ref in totals:
        total_ref[...] = jnp.zeros(total_ref.shape, jnp.float32)


def collect(parts, panels, slots, base):
    width = parts[0].shape[1]
    total = slots * CORES * len(parts)
    assert base ** (panels * slots) < 2**24
    vmem = pl.BlockSpec(memory_space=pltpu.VMEM)
    return pl.pallas_call(
        functools.partial(collect_kernel, panels, slots, base),
        out_shape=[
            pltpu.SMEM((panels, total), jnp.int32),
            pltpu.VMEM((panels, total, width, width), parts[0].dtype),
            *(pltpu.VMEM(((last - first) * width, NJ * width), jnp.float32) for first, last in GROUPS),
        ],
        in_specs=[vmem] * len(parts),
        out_specs=[pl.BlockSpec(memory_space=pltpu.SMEM)] + [vmem] * (1 + len(GROUPS)),
        compiler_params=pltpu.CompilerParams(vmem_limit_bytes=VMEM_LIMIT),
        name="collect",
    )(*map(in_vmem, parts))


def chunk_updates(codes_ref, hops, order, rows_held, slots):
    me = lax.axis_index("row")
    inverse = [order.index(at) for at in range(len(order))]
    here = pick(inverse, me)
    found = []
    for panel, way in hops:
        source = pick(order, lax.rem(here + len(order) - way, len(order)))
        owner, held = source // rows_held, lax.rem(source, rows_held)
        for at in range(slots):
            slot = owner * slots + at
            code = codes_ref[panel, slot]
            live = (code >= 0) & (code // NJ == held)
            found.append((live, slot, lax.rem(jnp.maximum(code, 0), NJ)))
    return found


def columns_of(found):
    hits = []
    for column in range(NJ):
        hit = jnp.bool_(False)
        for live, _, at in found:
            hit = hit | (live & (at == column))
        hits.append(hit)
    return hits


def fold_kernel(first, hops, later, order, rows_held, slots, band, codes_ref, ints_ref, *refs):
    chunks, rest = refs[: len(hops)], refs[len(hops) :]
    width = ints_ref.shape[2]
    found = chunk_updates(codes_ref, hops, order, rows_held, slots)
    if later is None:
        total_ref = rest[-1]
    elif later:
        total_ref, out_ref, sem = rest[-3], rest[-2], rest[-1]
        ready = [jnp.logical_not(hit) for hit in columns_of(chunk_updates(codes_ref, later, order, rows_held, slots))]
    else:
        total_ref, out_ref, sem = rest[0], rest[-2], rest[-1]
    rows = pl.ds(band[0], band[1])

    def send(column):
        cols = pl.ds(pl.multiple_of(column * width, width), width)
        return pltpu.make_async_copy(
            total_ref.at[rows, cols], out_ref.at[rows, cols], sem.at[column]
        )

    if first:
        total_ref[...] = jnp.zeros(total_ref.shape, jnp.float32)
    if later:
        hits = columns_of(found)
        for column in range(NJ):

            @pl.when(ready[column] & jnp.logical_not(hits[column]))
            def _():
                send(column).start()

    final = []
    for index, (live, slot, column) in enumerate(found):
        panel, chunk = hops[index // slots][0], chunks[index // slots]
        again = jnp.bool_(False)
        for other, _, at in found[index + 1 :]:
            again = again | (other & (at == column))
        final.append(live & jnp.logical_not(again))

        @pl.when(live)
        def _():
            cols = pl.ds(pl.multiple_of(column * width, width), width)
            total_ref[rows, cols] += jnp.dot(
                chunk[...], ints_ref[panel, slot], preferred_element_type=jnp.float32
            )

        if later is not None and not later:

            @pl.when(final[-1])
            def _():
                send(column).start()

    if later:
        for column in range(NJ):

            @pl.when(ready[column] & hits[column])
            def _():
                send(column).start()

        for column in range(NJ):

            @pl.when(ready[column])
            def _():
                send(column).wait()

    elif later is not None:
        for done, (_, _, column) in zip(final, found):

            @pl.when(done)
            def _():
                send(column).wait()


def fold(codes, ints, chunks, hops, later, total, out, order, rows_held, slots, band, whole):
    first = total is None
    rows, width = chunks[0].shape
    vmem = pl.BlockSpec(memory_space=pltpu.VMEM)
    anywhere = pl.BlockSpec(memory_space=pl.ANY)
    operands = [pltpu.with_memory_space_constraint(codes, pltpu.SMEM), in_vmem(ints), *map(in_vmem, chunks)]
    in_specs = [pl.BlockSpec(memory_space=pltpu.SMEM)] + [vmem] * (1 + len(chunks))
    aliases, scratch, out_shapes, out_specs = {}, [], [], []
    if not first:
        operands.append(in_vmem(total))
        in_specs.append(vmem)
    if later is None or later:
        if not first:
            aliases[len(operands) - 1] = 0
        out_shapes.append(pltpu.VMEM(total.shape, jnp.float32))
        out_specs.append(vmem)
    if later is not None:
        if out is not None:
            aliases[len(operands)] = len(out_shapes)
            operands.append(out)
            in_specs.append(anywhere)
        out_shapes.append(jax.ShapeDtypeStruct(whole, jnp.float32))
        out_specs.append(anywhere)
        scratch = [pltpu.SemaphoreType.DMA((NJ,))]
    return pl.pallas_call(
        functools.partial(fold_kernel, first, hops, later, order, rows_held, slots, band),
        out_shape=out_shapes,
        in_specs=in_specs,
        out_specs=out_specs,
        scratch_shapes=scratch,
        input_output_aliases=aliases,
        compiler_params=pltpu.CompilerParams(vmem_limit_bytes=VMEM_LIMIT),
        cost_estimate=pl.CostEstimate(
            flops=2 * rows * width * width * len(hops) * slots,
            bytes_accessed=rows * NJ * width * 4,
            transcendentals=0,
        ),
        name="fold",
    )(*operands)


def body(amp_tiles, amp_rows, int_tiles, int_codes):
    n_row, n_col = lax.axis_size("row"), lax.axis_size("col")
    rows_held = n_row // n_col
    panels, slots, width = int_tiles.shape[0], int_tiles.shape[1], int_tiles.shape[3]
    across = n_col // CORES
    order = grid_cycle(n_row // across, across)[::-1]
    forth = [(order[at], order[(at + 1) % n_row]) for at in range(n_row)]
    ways = [forth, [(b, a) for a, b in forth]]

    swap = [(c, c // CORES * CORES + (c + 1) % CORES) for c in range(n_col)]
    whole = (MI * width, NJ * width)
    placed = place(amp_tiles, amp_rows, int_tiles, int_codes)
    streams, parcel = placed[:-1], placed[-1]
    parts = [join([parcel, lax.ppermute(parcel, "col", swap)])]
    for shift in range(1, n_col // CORES):
        moved = lax.optimization_barrier((parts[0], parts[-1]))[0] if shift > 1 else parts[0]
        parts.append(lax.ppermute(moved, "col", [(c, (c + shift * CORES) % n_col) for c in range(n_col)]))
    codes, ints, total = collect(parts, panels, slots, rows_held * NJ + 1)
    rows = MI * width

    def add(chunks, later, total, out, band):
        tags = [tag for tag, _ in chunks]
        made = fold(
            codes, ints, [chunk for _, chunk in chunks], tags, later, total, out, order, rows_held, slots, band, whole
        )
        return made if later else made[0]

    far = n_row // 2
    lead = [(panel % 2, panel) for panel in range(panels)]
    rest = [(1 - panel % 2, panel) for panel in range(panels)]

    def tag(way, panel, hop):
        return (panel, hop if way == 0 else n_row - hop)

    held = {(way, panel): streams[panel] for way in range(2) for panel in range(panels)}
    have = [((panel, 0), streams[panel]) for panel in range(panels)]
    for hop in range(1, far):
        if hop == far - 1:
            total = early = add(have, None, total, None, (0, rows))
            have = []
        for one in lead + rest:
            if hop < far - 1 or far - 1 <= n_row - 1 - far or one in lead:
                held[one] = lax.ppermute(held[one], "row", ways[one[0]])
                have.append((tag(*one, hop), held[one]))
    last = [lax.optimization_barrier((early, held[one]))[1] for one in lead]
    pieces = split(last)
    later = [tag(*one, far) for one in lead]
    ends = [[lax.ppermute(piece, "row", ways[one[0]]) for one, piece in zip(lead, half)] for half in pieces]
    total, out = add(have, later, total, None, (0, rows))
    for at, half in enumerate(ends):
        out = add(list(zip(later, half)), [], total, out, (at * rows // 2, rows // 2))
    return out


def solution(mesh):
    return jax.shard_map(
        body,
        mesh=mesh,
        in_specs=(
            P(None, "col", "row", None, None),
            P(None, "col", "row"),
            P(None, "col", "row", None, None),
            P(None, "col", "row"),
        ),
        out_specs=P("col", "row"),
        check_vma=False,
    )
```

```python
import functools

import jax
import jax.numpy as jnp
from jax import lax
from jax.experimental import pallas as pl
from jax.experimental.pallas import tpu as pltpu
from jax.sharding import PartitionSpec as P

MI = 4
NJ = 6
CORES = 2
GROUPS = ((0, MI),)
LINES = 16
PIECES = (6, 2)
VMEM_LIMIT = 8 * 1024 * 1024


def grid_cycle(depth, across):
    order = [z * across for z in range(depth)]
    for turn, z in enumerate(reversed(range(depth))):
        xs = range(1, across) if turn % 2 == 0 else range(across - 1, 0, -1)
        order += [z * across + x for x in xs]
    return order


def pick(table, index):
    value = jnp.int32(table[0])
    for at in range(1, len(table)):
        value = jnp.where(index == at, jnp.int32(table[at]), value)
    return value


def in_vmem(value):
    return pltpu.with_memory_space_constraint(value, pltpu.VMEM)


def in_hbm(value):
    return pltpu.with_memory_space_constraint(value, pltpu.HBM)


def place_kernel(rows_hbm, codes_hbm, tiles_hbm, ints_hbm, *rest):
    placed, parcel_ref = rest[: -1 - 6], rest[-1 - 6]
    rows_ref, codes_ref, tiles_ref, small_sem, tiles_sem, ints_sem = rest[-6:]
    panels, slots, width = tiles_ref.shape[0], tiles_ref.shape[1], tiles_ref.shape[2]
    held = ints_hbm.shape[1]
    small = [
        pltpu.make_async_copy(rows_hbm, rows_ref, small_sem.at[0]),
        pltpu.make_async_copy(codes_hbm, codes_ref, small_sem.at[1]),
    ]
    tiles = [
        pltpu.make_async_copy(tiles_hbm.at[panel, 0], tiles_ref.at[panel], tiles_sem.at[panel])
        for panel in range(panels)
    ]
    parcels = [
        pltpu.make_async_copy(
            ints_hbm.at[panel, at, 0],
            parcel_ref.at[pl.ds((panel * held + at) * width, width)],
            ints_sem.at[panel, at],
        )
        for panel in range(panels)
        for at in range(held)
    ]
    for copy in small + tiles + parcels:
        copy.start()
    for copy in small:
        copy.wait()
    lines = lax.broadcasted_iota(jnp.int32, (LINES, width), 0)
    labels = jnp.zeros((LINES, width), jnp.float32)
    for panel in range(panels):
        for at in range(held):
            code = codes_ref[panel, 0, at].astype(jnp.float32)
            labels = jnp.where(lines == panel * held + at, code, labels)
    parcel_ref[pl.ds(panels * held * width, LINES)] = labels.astype(parcel_ref.dtype)
    for panel in range(panels):
        tiles[panel].wait()
        for group, (first, last) in enumerate(GROUPS):
            for row in range(first, last):
                slot = jnp.int32(-1)
                for at in range(slots):
                    slot = jnp.where(rows_ref[panel, 0, at] == row, at, slot)
                spot = placed[group * panels + panel].at[pl.ds((row - first) * width, width)]

                @pl.when(slot >= 0)
                def _():
                    spot[...] = tiles_ref[panel, jnp.maximum(slot, 0)]

                @pl.when(slot < 0)
                def _():
                    spot[...] = jnp.zeros(spot.shape, spot.dtype)

    for copy in parcels:
        copy.wait()


def place(amp_tiles, amp_rows, int_tiles, int_codes):
    panels, held, slots, width = amp_tiles.shape[0], int_tiles.shape[1], amp_tiles.shape[2], amp_tiles.shape[3]
    codes = jnp.transpose(int_codes, (0, 2, 1))
    shapes = [
        pltpu.VMEM(((last - first) * width, width), amp_tiles.dtype)
        for first, last in GROUPS
        for _ in range(panels)
    ]
    shapes.append(pltpu.VMEM((panels * held * width + LINES, width), int_tiles.dtype))
    return pl.pallas_call(
        place_kernel,
        out_shape=shapes,
        in_specs=[pl.BlockSpec(memory_space=pl.ANY)] * 4,
        out_specs=[pl.BlockSpec(memory_space=pltpu.VMEM)] * len(shapes),
        scratch_shapes=[
            pltpu.SMEM(amp_rows.shape, jnp.int32),
            pltpu.SMEM(codes.shape, jnp.int32),
            pltpu.VMEM((panels, slots, width, width), amp_tiles.dtype),
            pltpu.SemaphoreType.DMA((2,)),
            pltpu.SemaphoreType.DMA((panels,)),
            pltpu.SemaphoreType.DMA((panels, held)),
        ],
        compiler_params=pltpu.CompilerParams(vmem_limit_bytes=VMEM_LIMIT),
        name="place",
    )(in_hbm(amp_rows), in_hbm(codes), in_hbm(amp_tiles), in_hbm(int_tiles))


def split_kernel(*refs):
    count = len(refs) // (1 + len(PIECES))
    for at, ref in enumerate(refs[:count]):
        first = 0
        for piece in range(len(PIECES)):
            part = refs[count * (1 + piece) + at]
            part[...] = ref[pl.ds(first, part.shape[0])]
            first += part.shape[0]


def split(chunks):
    rows, width = chunks[0].shape
    vmem = pl.BlockSpec(memory_space=pltpu.VMEM)
    shapes = [pltpu.VMEM((rows * eighths // 8, width), chunks[0].dtype) for eighths in PIECES for _ in chunks]
    made = pl.pallas_call(
        split_kernel,
        out_shape=shapes,
        in_specs=[vmem] * len(chunks),
        out_specs=[vmem] * len(shapes),
        compiler_params=pltpu.CompilerParams(vmem_limit_bytes=VMEM_LIMIT),
        name="split",
    )(*map(in_vmem, chunks))
    return [made[at : at + len(chunks)] for at in range(0, len(made), len(chunks))]


def join_kernel(*refs):
    size = refs[0].shape[0]
    for at, ref in enumerate(refs[:-1]):
        refs[-1][pl.ds(at * size, size)] = ref[...]


def join(parts):
    size, width = parts[0].shape
    vmem = pl.BlockSpec(memory_space=pltpu.VMEM)
    return pl.pallas_call(
        join_kernel,
        out_shape=pltpu.VMEM((size * len(parts), width), parts[0].dtype),
        in_specs=[vmem] * len(parts),
        out_specs=vmem,
        compiler_params=pltpu.CompilerParams(vmem_limit_bytes=VMEM_LIMIT),
        name="join",
    )(*map(in_vmem, parts))


def collect_kernel(panels, slots, base, *refs):
    refs, totals = refs[: -len(GROUPS)], refs[-len(GROUPS) :]
    joined, codes_ref, out_ref = refs[:-2], refs[-2], refs[-1]
    width = joined[0].shape[1]
    size = panels * slots * width + LINES
    depth = len(joined)
    parts = [joined[shift].at[pl.ds(flip * size, size)] for shift in range(depth) for flip in range(CORES)]
    col = lax.axis_index("col")
    y, core = col // CORES, lax.rem(col, CORES)
    owners = []
    for at, part in enumerate(parts):
        shift, flip = at // CORES, at % CORES
        owner = lax.rem(y + depth - shift, depth) * CORES + lax.rem(core + flip, CORES)
        owners.append(owner)
        for panel in range(panels):
            for slot in range(slots):
                out_ref[panel, owner * slots + slot] = part[pl.ds((panel * slots + slot) * width, width)]
    lines = lax.broadcasted_iota(jnp.int32, (LINES, width), 0)
    scale = jnp.zeros((LINES, width), jnp.float32)
    for at in range(panels * slots):
        scale = jnp.where(lines == at, float(base**at), scale)
    for owner, part in zip(owners, parts):
        labels = part[pl.ds(panels * slots * width, LINES), pl.ds(0, 128)].astype(jnp.float32) + 1.0
        number = jnp.sum(labels * scale[:, :128], axis=0, keepdims=True)
        digits = jnp.max(number).astype(jnp.int32)
        for panel in range(panels):
            for slot in range(slots):
                codes_ref[panel, owner * slots + slot] = lax.rem(digits, base) - 1
                digits = digits // base
    for total_ref in totals:
        total_ref[...] = jnp.zeros(total_ref.shape, jnp.float32)


def collect(parts, panels, slots, base):
    width = parts[0].shape[1]
    total = slots * CORES * len(parts)
    assert base ** (panels * slots) < 2**24
    vmem = pl.BlockSpec(memory_space=pltpu.VMEM)
    return pl.pallas_call(
        functools.partial(collect_kernel, panels, slots, base),
        out_shape=[
            pltpu.SMEM((panels, total), jnp.int32),
            pltpu.VMEM((panels, total, width, width), parts[0].dtype),
            *(pltpu.VMEM(((last - first) * width, NJ * width), jnp.float32) for first, last in GROUPS),
        ],
        in_specs=[vmem] * len(parts),
        out_specs=[pl.BlockSpec(memory_space=pltpu.SMEM)] + [vmem] * (1 + len(GROUPS)),
        compiler_params=pltpu.CompilerParams(vmem_limit_bytes=VMEM_LIMIT),
        name="collect",
    )(*map(in_vmem, parts))


def chunk_updates(codes_ref, hops, order, rows_held, slots):
    me = lax.axis_index("row")
    inverse = [order.index(at) for at in range(len(order))]
    here = pick(inverse, me)
    found = []
    for panel, way in hops:
        source = pick(order, lax.rem(here + len(order) - way, len(order)))
        owner, held = source // rows_held, lax.rem(source, rows_held)
        for at in range(slots):
            slot = owner * slots + at
            code = codes_ref[panel, slot]
            live = (code >= 0) & (code // NJ == held)
            found.append((live, slot, lax.rem(jnp.maximum(code, 0), NJ)))
    return found


def columns_of(found):
    hits = []
    for column in range(NJ):
        hit = jnp.bool_(False)
        for live, _, at in found:
            hit = hit | (live & (at == column))
        hits.append(hit)
    return hits


def fold_kernel(first, hops, later, order, rows_held, slots, band, codes_ref, ints_ref, *refs):
    chunks, rest = refs[: len(hops)], refs[len(hops) :]
    width = ints_ref.shape[2]
    found = chunk_updates(codes_ref, hops, order, rows_held, slots)
    if later is None:
        total_ref = rest[-1]
    elif later:
        total_ref, out_ref, sem = rest[-3], rest[-2], rest[-1]
        ready = [jnp.logical_not(hit) for hit in columns_of(chunk_updates(codes_ref, later, order, rows_held, slots))]
    else:
        total_ref, out_ref, sem = rest[0], rest[-2], rest[-1]
    rows = pl.ds(band[0], band[1])

    def send(column):
        cols = pl.ds(pl.multiple_of(column * width, width), width)
        return pltpu.make_async_copy(
            total_ref.at[rows, cols], out_ref.at[rows, cols], sem.at[column]
        )

    if first:
        total_ref[...] = jnp.zeros(total_ref.shape, jnp.float32)
    if later:
        hits = columns_of(found)
        for column in range(NJ):

            @pl.when(ready[column] & jnp.logical_not(hits[column]))
            def _():
                send(column).start()

    final = []
    for index, (live, slot, column) in enumerate(found):
        panel, chunk = hops[index // slots][0], chunks[index // slots]
        again = jnp.bool_(False)
        for other, _, at in found[index + 1 :]:
            again = again | (other & (at == column))
        final.append(live & jnp.logical_not(again))

        @pl.when(live)
        def _():
            cols = pl.ds(pl.multiple_of(column * width, width), width)
            total_ref[rows, cols] += jnp.dot(
                chunk[...], ints_ref[panel, slot], preferred_element_type=jnp.float32
            )

        if later is not None and not later:

            @pl.when(final[-1])
            def _():
                send(column).start()

    if later:
        for column in range(NJ):

            @pl.when(ready[column] & hits[column])
            def _():
                send(column).start()

        for column in range(NJ):

            @pl.when(ready[column])
            def _():
                send(column).wait()

    elif later is not None:
        for done, (_, _, column) in zip(final, found):

            @pl.when(done)
            def _():
                send(column).wait()


def fold(codes, ints, chunks, hops, later, total, out, order, rows_held, slots, band, whole):
    first = total is None
    rows, width = chunks[0].shape
    vmem = pl.BlockSpec(memory_space=pltpu.VMEM)
    anywhere = pl.BlockSpec(memory_space=pl.ANY)
    operands = [pltpu.with_memory_space_constraint(codes, pltpu.SMEM), in_vmem(ints), *map(in_vmem, chunks)]
    in_specs = [pl.BlockSpec(memory_space=pltpu.SMEM)] + [vmem] * (1 + len(chunks))
    aliases, scratch, out_shapes, out_specs = {}, [], [], []
    if not first:
        operands.append(in_vmem(total))
        in_specs.append(vmem)
    if later is None or later:
        if not first:
            aliases[len(operands) - 1] = 0
        out_shapes.append(pltpu.VMEM(total.shape, jnp.float32))
        out_specs.append(vmem)
    if later is not None:
        if out is not None:
            aliases[len(operands)] = len(out_shapes)
            operands.append(out)
            in_specs.append(anywhere)
        out_shapes.append(jax.ShapeDtypeStruct(whole, jnp.float32))
        out_specs.append(anywhere)
        scratch = [pltpu.SemaphoreType.DMA((NJ,))]
    return pl.pallas_call(
        functools.partial(fold_kernel, first, hops, later, order, rows_held, slots, band),
        out_shape=out_shapes,
        in_specs=in_specs,
        out_specs=out_specs,
        scratch_shapes=scratch,
        input_output_aliases=aliases,
        compiler_params=pltpu.CompilerParams(vmem_limit_bytes=VMEM_LIMIT),
        cost_estimate=pl.CostEstimate(
            flops=2 * rows * width * width * len(hops) * slots,
            bytes_accessed=rows * NJ * width * 4,
            transcendentals=0,
        ),
        name="fold",
    )(*operands)


def body(amp_tiles, amp_rows, int_tiles, int_codes):
    n_row, n_col = lax.axis_size("row"), lax.axis_size("col")
    rows_held = n_row // n_col
    panels, slots, width = int_tiles.shape[0], int_tiles.shape[1], int_tiles.shape[3]
    across = n_col // CORES
    order = grid_cycle(n_row // across, across)[::-1]
    forth = [(order[at], order[(at + 1) % n_row]) for at in range(n_row)]
    ways = [forth, [(b, a) for a, b in forth]]

    swap = [(c, c // CORES * CORES + (c + 1) % CORES) for c in range(n_col)]
    whole = (MI * width, NJ * width)
    placed = place(amp_tiles, amp_rows, int_tiles, int_codes)
    streams, parcel = placed[:-1], placed[-1]
    parts = [join([parcel, lax.ppermute(parcel, "col", swap)])]
    for shift in range(1, n_col // CORES):
        moved = lax.optimization_barrier((parts[0], parts[-1]))[0] if shift > 1 else parts[0]
        parts.append(lax.ppermute(moved, "col", [(c, (c + shift * CORES) % n_col) for c in range(n_col)]))
    codes, ints, total = collect(parts, panels, slots, rows_held * NJ + 1)
    rows = MI * width

    def add(chunks, later, total, out, band):
        tags = [tag for tag, _ in chunks]
        made = fold(
            codes, ints, [chunk for _, chunk in chunks], tags, later, total, out, order, rows_held, slots, band, whole
        )
        return made if later else made[0]

    far = n_row // 2
    lead = [(panel % 2, panel) for panel in range(panels)]
    rest = [(1 - panel % 2, panel) for panel in range(panels)]

    def tag(way, panel, hop):
        return (panel, hop if way == 0 else n_row - hop)

    held = {(way, panel): streams[panel] for way in range(2) for panel in range(panels)}
    have = [((panel, 0), streams[panel]) for panel in range(panels)]
    for hop in range(1, far):
        if hop == far - 1:
            total = early = add(have, None, total, None, (0, rows))
            have = []
        for one in lead + rest:
            if hop < far - 1 or far - 1 <= n_row - 1 - far or one in lead:
                held[one] = lax.ppermute(held[one], "row", ways[one[0]])
                have.append((tag(*one, hop), held[one]))
    last = [lax.optimization_barrier((early, held[one]))[1] for one in lead]
    pieces = split(last)
    later = [tag(*one, far) for one in lead]
    ends = [[lax.ppermute(part, "row", ways[one[0]]) for one, part in zip(lead, piece)] for piece in pieces]
    total, out = add(have, later, total, None, (0, rows))
    first = 0
    for piece, eighths in zip(ends, PIECES):
        out = add(list(zip(later, piece)), [], total, out, (first, rows * eighths // 8))
        first += rows * eighths // 8
    return out


def solution(mesh):
    return jax.shard_map(
        body,
        mesh=mesh,
        in_specs=(
            P(None, "col", "row", None, None),
            P(None, "col", "row"),
            P(None, "col", "row", None, None),
            P(None, "col", "row"),
        ),
        out_specs=P("col", "row"),
        check_vma=False,
    )
```

```python
import functools

import jax
import jax.numpy as jnp
from jax import lax
from jax.experimental import pallas as pl
from jax.experimental.pallas import tpu as pltpu
from jax.sharding import PartitionSpec as P

MI = 4
NJ = 6
CORES = 2
GROUPS = ((0, MI),)
LINES = 16
PIECES = (6, 2)
VMEM_LIMIT = 8 * 1024 * 1024


def grid_cycle(depth, across):
    order = [z * across for z in range(depth)]
    for turn, z in enumerate(reversed(range(depth))):
        xs = range(1, across) if turn % 2 == 0 else range(across - 1, 0, -1)
        order += [z * across + x for x in xs]
    return order


def pick(table, index):
    value = jnp.int32(table[0])
    for at in range(1, len(table)):
        value = jnp.where(index == at, jnp.int32(table[at]), value)
    return value


def in_vmem(value):
    return pltpu.with_memory_space_constraint(value, pltpu.VMEM)


def in_hbm(value):
    return pltpu.with_memory_space_constraint(value, pltpu.HBM)


def place_kernel(rows_hbm, codes_hbm, tiles_hbm, ints_hbm, *rest):
    placed, parcel_ref = rest[: -1 - 6], rest[-1 - 6]
    rows_ref, codes_ref, tiles_ref, small_sem, tiles_sem, ints_sem = rest[-6:]
    panels, slots, width = tiles_ref.shape[0], tiles_ref.shape[1], tiles_ref.shape[2]
    held = ints_hbm.shape[1]
    small = [
        pltpu.make_async_copy(rows_hbm, rows_ref, small_sem.at[0]),
        pltpu.make_async_copy(codes_hbm, codes_ref, small_sem.at[1]),
    ]
    tiles = [
        pltpu.make_async_copy(tiles_hbm.at[panel, 0], tiles_ref.at[panel], tiles_sem.at[panel])
        for panel in range(panels)
    ]
    parcels = [
        pltpu.make_async_copy(
            ints_hbm.at[panel, at, 0],
            parcel_ref.at[pl.ds((panel * held + at) * width, width)],
            ints_sem.at[panel, at],
        )
        for panel in range(panels)
        for at in range(held)
    ]
    for copy in small + tiles + parcels:
        copy.start()
    for copy in small:
        copy.wait()
    lines = lax.broadcasted_iota(jnp.int32, (LINES, width), 0)
    labels = jnp.zeros((LINES, width), jnp.float32)
    for panel in range(panels):
        for at in range(held):
            code = codes_ref[panel, 0, at].astype(jnp.float32)
            labels = jnp.where(lines == panel * held + at, code, labels)
    parcel_ref[pl.ds(panels * held * width, LINES)] = labels.astype(parcel_ref.dtype)
    for panel in range(panels):
        tiles[panel].wait()
        for group, (first, last) in enumerate(GROUPS):
            for row in range(first, last):
                slot = jnp.int32(-1)
                for at in range(slots):
                    slot = jnp.where(rows_ref[panel, 0, at] == row, at, slot)
                spot = placed[group * panels + panel].at[pl.ds((row - first) * width, width)]

                @pl.when(slot >= 0)
                def _():
                    spot[...] = tiles_ref[panel, jnp.maximum(slot, 0)]

                @pl.when(slot < 0)
                def _():
                    spot[...] = jnp.zeros(spot.shape, spot.dtype)

    for copy in parcels:
        copy.wait()


def place(amp_tiles, amp_rows, int_tiles, int_codes):
    panels, held, slots, width = amp_tiles.shape[0], int_tiles.shape[1], amp_tiles.shape[2], amp_tiles.shape[3]
    codes = jnp.transpose(int_codes, (0, 2, 1))
    shapes = [
        pltpu.VMEM(((last - first) * width, width), amp_tiles.dtype)
        for first, last in GROUPS
        for _ in range(panels)
    ]
    shapes.append(pltpu.VMEM((panels * held * width + LINES, width), int_tiles.dtype))
    return pl.pallas_call(
        place_kernel,
        out_shape=shapes,
        in_specs=[pl.BlockSpec(memory_space=pl.ANY)] * 4,
        out_specs=[pl.BlockSpec(memory_space=pltpu.VMEM)] * len(shapes),
        scratch_shapes=[
            pltpu.SMEM(amp_rows.shape, jnp.int32),
            pltpu.SMEM(codes.shape, jnp.int32),
            pltpu.VMEM((panels, slots, width, width), amp_tiles.dtype),
            pltpu.SemaphoreType.DMA((2,)),
            pltpu.SemaphoreType.DMA((panels,)),
            pltpu.SemaphoreType.DMA((panels, held)),
        ],
        compiler_params=pltpu.CompilerParams(vmem_limit_bytes=VMEM_LIMIT),
        name="place",
    )(in_hbm(amp_rows), in_hbm(codes), in_hbm(amp_tiles), in_hbm(int_tiles))


def split_kernel(*refs):
    count = len(refs) // (1 + len(PIECES))
    for at, ref in enumerate(refs[:count]):
        first = 0
        for piece in range(len(PIECES)):
            part = refs[count * (1 + piece) + at]
            part[...] = ref[pl.ds(first, part.shape[0])]
            first += part.shape[0]


def split(chunks):
    rows, width = chunks[0].shape
    vmem = pl.BlockSpec(memory_space=pltpu.VMEM)
    shapes = [pltpu.VMEM((rows * eighths // 8, width), chunks[0].dtype) for eighths in PIECES for _ in chunks]
    made = pl.pallas_call(
        split_kernel,
        out_shape=shapes,
        in_specs=[vmem] * len(chunks),
        out_specs=[vmem] * len(shapes),
        compiler_params=pltpu.CompilerParams(vmem_limit_bytes=VMEM_LIMIT),
        name="split",
    )(*map(in_vmem, chunks))
    return [made[at : at + len(chunks)] for at in range(0, len(made), len(chunks))]


def join_kernel(*refs):
    size = refs[0].shape[0]
    for at, ref in enumerate(refs[:-1]):
        refs[-1][pl.ds(at * size, size)] = ref[...]


def join(parts):
    size, width = parts[0].shape
    vmem = pl.BlockSpec(memory_space=pltpu.VMEM)
    return pl.pallas_call(
        join_kernel,
        out_shape=pltpu.VMEM((size * len(parts), width), parts[0].dtype),
        in_specs=[vmem] * len(parts),
        out_specs=vmem,
        compiler_params=pltpu.CompilerParams(vmem_limit_bytes=VMEM_LIMIT),
        name="join",
    )(*map(in_vmem, parts))


def collect_kernel(panels, slots, base, *refs):
    refs, totals = refs[: -len(GROUPS)], refs[-len(GROUPS) :]
    joined, codes_ref, out_ref = refs[:-2], refs[-2], refs[-1]
    width = joined[0].shape[1]
    size = panels * slots * width + LINES
    depth = len(joined)
    parts = [joined[shift].at[pl.ds(flip * size, size)] for shift in range(depth) for flip in range(CORES)]
    col = lax.axis_index("col")
    y, core = col // CORES, lax.rem(col, CORES)
    owners = []
    for at, part in enumerate(parts):
        shift, flip = at // CORES, at % CORES
        owner = lax.rem(y + depth - shift, depth) * CORES + lax.rem(core + flip, CORES)
        owners.append(owner)
        for panel in range(panels):
            for slot in range(slots):
                out_ref[panel, owner * slots + slot] = part[pl.ds((panel * slots + slot) * width, width)]
    lines = lax.broadcasted_iota(jnp.int32, (LINES, width), 0)
    scale = jnp.zeros((LINES, width), jnp.float32)
    for at in range(panels * slots):
        scale = jnp.where(lines == at, float(base**at), scale)
    for owner, part in zip(owners, parts):
        labels = part[pl.ds(panels * slots * width, LINES), pl.ds(0, 128)].astype(jnp.float32) + 1.0
        number = jnp.sum(labels * scale[:, :128], axis=0, keepdims=True)
        digits = jnp.max(number).astype(jnp.int32)
        for panel in range(panels):
            for slot in range(slots):
                codes_ref[panel, owner * slots + slot] = lax.rem(digits, base) - 1
                digits = digits // base
    for total_ref in totals:
        total_ref[...] = jnp.zeros(total_ref.shape, jnp.float32)


def collect(parts, panels, slots, base):
    width = parts[0].shape[1]
    total = slots * CORES * len(parts)
    assert base ** (panels * slots) < 2**24
    vmem = pl.BlockSpec(memory_space=pltpu.VMEM)
    return pl.pallas_call(
        functools.partial(collect_kernel, panels, slots, base),
        out_shape=[
            pltpu.SMEM((panels, total), jnp.int32),
            pltpu.VMEM((panels, total, width, width), parts[0].dtype),
            *(pltpu.VMEM(((last - first) * width, NJ * width), jnp.float32) for first, last in GROUPS),
        ],
        in_specs=[vmem] * len(parts),
        out_specs=[pl.BlockSpec(memory_space=pltpu.SMEM)] + [vmem] * (1 + len(GROUPS)),
        compiler_params=pltpu.CompilerParams(vmem_limit_bytes=VMEM_LIMIT),
        name="collect",
    )(*map(in_vmem, parts))


def chunk_updates(codes_ref, hops, order, rows_held, slots):
    me = lax.axis_index("row")
    inverse = [order.index(at) for at in range(len(order))]
    here = pick(inverse, me)
    found = []
    for panel, way in hops:
        source = pick(order, lax.rem(here + len(order) - way, len(order)))
        owner, held = source // rows_held, lax.rem(source, rows_held)
        for at in range(slots):
            slot = owner * slots + at
            code = codes_ref[panel, slot]
            live = (code >= 0) & (code // NJ == held)
            found.append((live, slot, lax.rem(jnp.maximum(code, 0), NJ)))
    return found


def columns_of(found):
    hits = []
    for column in range(NJ):
        hit = jnp.bool_(False)
        for live, _, at in found:
            hit = hit | (live & (at == column))
        hits.append(hit)
    return hits


def fold_kernel(first, hops, later, order, rows_held, slots, band, codes_ref, ints_ref, *refs):
    chunks, rest = refs[: len(hops)], refs[len(hops) :]
    width = ints_ref.shape[2]
    found = chunk_updates(codes_ref, hops, order, rows_held, slots)
    if later is None:
        total_ref = rest[-1]
    elif later:
        total_ref, out_ref, sem = rest[-3], rest[-2], rest[-1]
        ready = [jnp.logical_not(hit) for hit in columns_of(chunk_updates(codes_ref, later, order, rows_held, slots))]
    else:
        total_ref, out_ref, sem = rest[0], rest[-2], rest[-1]
    rows = pl.ds(band[0], band[1])

    def send(column):
        cols = pl.ds(pl.multiple_of(column * width, width), width)
        return pltpu.make_async_copy(
            total_ref.at[rows, cols], out_ref.at[rows, cols], sem.at[column]
        )

    if first:
        total_ref[...] = jnp.zeros(total_ref.shape, jnp.float32)
    if later:
        hits = columns_of(found)
        for column in range(NJ):

            @pl.when(ready[column] & jnp.logical_not(hits[column]))
            def _():
                send(column).start()

    final = []
    for index, (live, slot, column) in enumerate(found):
        panel, chunk = hops[index // slots][0], chunks[index // slots]
        again = jnp.bool_(False)
        for other, _, at in found[index + 1 :]:
            again = again | (other & (at == column))
        final.append(live & jnp.logical_not(again))

        @pl.when(live)
        def _():
            cols = pl.ds(pl.multiple_of(column * width, width), width)
            total_ref[rows, cols] += jnp.dot(
                chunk[...], ints_ref[panel, slot], preferred_element_type=jnp.float32
            )

        if later is not None and not later:

            @pl.when(final[-1])
            def _():
                send(column).start()

    if later:
        for column in range(NJ):

            @pl.when(ready[column] & hits[column])
            def _():
                send(column).start()

        for column in range(NJ):

            @pl.when(ready[column])
            def _():
                send(column).wait()

    elif later is not None:
        for done, (_, _, column) in zip(final, found):

            @pl.when(done)
            def _():
                send(column).wait()


def fold(codes, ints, chunks, hops, later, total, out, order, rows_held, slots, band, whole):
    first = total is None
    rows, width = chunks[0].shape
    vmem = pl.BlockSpec(memory_space=pltpu.VMEM)
    anywhere = pl.BlockSpec(memory_space=pl.ANY)
    operands = [pltpu.with_memory_space_constraint(codes, pltpu.SMEM), in_vmem(ints), *map(in_vmem, chunks)]
    in_specs = [pl.BlockSpec(memory_space=pltpu.SMEM)] + [vmem] * (1 + len(chunks))
    aliases, scratch, out_shapes, out_specs = {}, [], [], []
    if not first:
        operands.append(in_vmem(total))
        in_specs.append(vmem)
    if later is None or later:
        if not first:
            aliases[len(operands) - 1] = 0
        out_shapes.append(pltpu.VMEM(total.shape, jnp.float32))
        out_specs.append(vmem)
    if later is not None:
        if out is not None:
            aliases[len(operands)] = len(out_shapes)
            operands.append(out)
            in_specs.append(anywhere)
        out_shapes.append(jax.ShapeDtypeStruct(whole, jnp.float32))
        out_specs.append(anywhere)
        scratch = [pltpu.SemaphoreType.DMA((NJ,))]
    return pl.pallas_call(
        functools.partial(fold_kernel, first, hops, later, order, rows_held, slots, band),
        out_shape=out_shapes,
        in_specs=in_specs,
        out_specs=out_specs,
        scratch_shapes=scratch,
        input_output_aliases=aliases,
        compiler_params=pltpu.CompilerParams(vmem_limit_bytes=VMEM_LIMIT),
        cost_estimate=pl.CostEstimate(
            flops=2 * rows * width * width * len(hops) * slots,
            bytes_accessed=rows * NJ * width * 4,
            transcendentals=0,
        ),
        name="fold",
    )(*operands)


def body(amp_tiles, amp_rows, int_tiles, int_codes):
    n_row, n_col = lax.axis_size("row"), lax.axis_size("col")
    rows_held = n_row // n_col
    panels, slots, width = int_tiles.shape[0], int_tiles.shape[1], int_tiles.shape[3]
    across = n_col // CORES
    order = grid_cycle(n_row // across, across)[::-1]
    forth = [(order[at], order[(at + 1) % n_row]) for at in range(n_row)]
    ways = [forth, [(b, a) for a, b in forth]]

    swap = [(c, c // CORES * CORES + (c + 1) % CORES) for c in range(n_col)]
    whole = (MI * width, NJ * width)
    placed = place(amp_tiles, amp_rows, int_tiles, int_codes)
    streams, parcel = placed[:-1], placed[-1]
    parts = [join([parcel, lax.ppermute(parcel, "col", swap)])]
    for shift in range(1, n_col // CORES):
        moved = lax.optimization_barrier((parts[0], parts[-1]))[0] if shift > 1 else parts[0]
        parts.append(lax.ppermute(moved, "col", [(c, (c + shift * CORES) % n_col) for c in range(n_col)]))
    codes, ints, total = collect(parts, panels, slots, rows_held * NJ + 1)
    rows = MI * width

    def add(chunks, later, total, out, band):
        tags = [tag for tag, _ in chunks]
        made = fold(
            codes, ints, [chunk for _, chunk in chunks], tags, later, total, out, order, rows_held, slots, band, whole
        )
        return made if later else made[0]

    far = n_row // 2
    lead = [(panel % 2, panel) for panel in range(panels)]
    rest = [(1 - panel % 2, panel) for panel in range(panels)]

    def tag(way, panel, hop):
        return (panel, hop if way == 0 else n_row - hop)

    held = {(way, panel): streams[panel] for way in range(2) for panel in range(panels)}
    have = [((panel, 0), streams[panel]) for panel in range(panels)]
    for hop in range(1, far):
        if hop == far - 1:
            total = early = add(have, None, total, None, (0, rows))
            have = []
        for one in lead + rest:
            if hop < far - 1 or far - 1 <= n_row - 1 - far or one in lead:
                held[one] = lax.ppermute(held[one], "row", ways[one[0]])
                have.append((tag(*one, hop), held[one]))
    last = [held[one] for one in lead]
    pieces = split(last)
    later = [tag(*one, far) for one in lead]
    ends = [[lax.ppermute(part, "row", ways[one[0]]) for one, part in zip(lead, piece)] for piece in pieces]
    total, out = add(have, later, total, None, (0, rows))
    first = 0
    for piece, eighths in zip(ends, PIECES):
        out = add(list(zip(later, piece)), [], total, out, (first, rows * eighths // 8))
        first += rows * eighths // 8
    return out


def solution(mesh):
    return jax.shard_map(
        body,
        mesh=mesh,
        in_specs=(
            P(None, "col", "row", None, None),
            P(None, "col", "row"),
            P(None, "col", "row", None, None),
            P(None, "col", "row"),
        ),
        out_specs=P("col", "row"),
        check_vma=False,
    )
```

```python
import functools

import jax
import jax.numpy as jnp
from jax import lax
from jax.experimental import pallas as pl
from jax.experimental.pallas import tpu as pltpu
from jax.sharding import PartitionSpec as P

MI = 4
NJ = 6
CORES = 2
GROUPS = ((0, MI),)
LINES = 16
PIECES = (5, 3)
VMEM_LIMIT = 8 * 1024 * 1024


def grid_cycle(depth, across):
    order = [z * across for z in range(depth)]
    for turn, z in enumerate(reversed(range(depth))):
        xs = range(1, across) if turn % 2 == 0 else range(across - 1, 0, -1)
        order += [z * across + x for x in xs]
    return order


def pick(table, index):
    value = jnp.int32(table[0])
    for at in range(1, len(table)):
        value = jnp.where(index == at, jnp.int32(table[at]), value)
    return value


def in_vmem(value):
    return pltpu.with_memory_space_constraint(value, pltpu.VMEM)


def in_hbm(value):
    return pltpu.with_memory_space_constraint(value, pltpu.HBM)


def place_kernel(rows_hbm, codes_hbm, tiles_hbm, ints_hbm, *rest):
    placed, parcel_ref = rest[: -1 - 6], rest[-1 - 6]
    rows_ref, codes_ref, tiles_ref, small_sem, tiles_sem, ints_sem = rest[-6:]
    panels, slots, width = tiles_ref.shape[0], tiles_ref.shape[1], tiles_ref.shape[2]
    held = ints_hbm.shape[1]
    small = [
        pltpu.make_async_copy(rows_hbm, rows_ref, small_sem.at[0]),
        pltpu.make_async_copy(codes_hbm, codes_ref, small_sem.at[1]),
    ]
    tiles = [
        pltpu.make_async_copy(tiles_hbm.at[panel, 0], tiles_ref.at[panel], tiles_sem.at[panel])
        for panel in range(panels)
    ]
    parcels = [
        pltpu.make_async_copy(
            ints_hbm.at[panel, at, 0],
            parcel_ref.at[pl.ds((panel * held + at) * width, width)],
            ints_sem.at[panel, at],
        )
        for panel in range(panels)
        for at in range(held)
    ]
    for copy in small + tiles + parcels:
        copy.start()
    for copy in small:
        copy.wait()
    lines = lax.broadcasted_iota(jnp.int32, (LINES, width), 0)
    labels = jnp.zeros((LINES, width), jnp.float32)
    for panel in range(panels):
        for at in range(held):
            code = codes_ref[panel, 0, at].astype(jnp.float32)
            labels = jnp.where(lines == panel * held + at, code, labels)
    parcel_ref[pl.ds(panels * held * width, LINES)] = labels.astype(parcel_ref.dtype)
    for panel in range(panels):
        tiles[panel].wait()
        for group, (first, last) in enumerate(GROUPS):
            for row in range(first, last):
                slot = jnp.int32(-1)
                for at in range(slots):
                    slot = jnp.where(rows_ref[panel, 0, at] == row, at, slot)
                spot = placed[group * panels + panel].at[pl.ds((row - first) * width, width)]

                @pl.when(slot >= 0)
                def _():
                    spot[...] = tiles_ref[panel, jnp.maximum(slot, 0)]

                @pl.when(slot < 0)
                def _():
                    spot[...] = jnp.zeros(spot.shape, spot.dtype)

    for copy in parcels:
        copy.wait()


def place(amp_tiles, amp_rows, int_tiles, int_codes):
    panels, held, slots, width = amp_tiles.shape[0], int_tiles.shape[1], amp_tiles.shape[2], amp_tiles.shape[3]
    codes = jnp.transpose(int_codes, (0, 2, 1))
    shapes = [
        pltpu.VMEM(((last - first) * width, width), amp_tiles.dtype)
        for first, last in GROUPS
        for _ in range(panels)
    ]
    shapes.append(pltpu.VMEM((panels * held * width + LINES, width), int_tiles.dtype))
    return pl.pallas_call(
        place_kernel,
        out_shape=shapes,
        in_specs=[pl.BlockSpec(memory_space=pl.ANY)] * 4,
        out_specs=[pl.BlockSpec(memory_space=pltpu.VMEM)] * len(shapes),
        scratch_shapes=[
            pltpu.SMEM(amp_rows.shape, jnp.int32),
            pltpu.SMEM(codes.shape, jnp.int32),
            pltpu.VMEM((panels, slots, width, width), amp_tiles.dtype),
            pltpu.SemaphoreType.DMA((2,)),
            pltpu.SemaphoreType.DMA((panels,)),
            pltpu.SemaphoreType.DMA((panels, held)),
        ],
        compiler_params=pltpu.CompilerParams(vmem_limit_bytes=VMEM_LIMIT),
        name="place",
    )(in_hbm(amp_rows), in_hbm(codes), in_hbm(amp_tiles), in_hbm(int_tiles))


def split_kernel(*refs):
    count = len(refs) // (1 + len(PIECES))
    for at, ref in enumerate(refs[:count]):
        first = 0
        for piece in range(len(PIECES)):
            part = refs[count * (1 + piece) + at]
            part[...] = ref[pl.ds(first, part.shape[0])]
            first += part.shape[0]


def split(chunks):
    rows, width = chunks[0].shape
    vmem = pl.BlockSpec(memory_space=pltpu.VMEM)
    shapes = [pltpu.VMEM((rows * eighths // 8, width), chunks[0].dtype) for eighths in PIECES for _ in chunks]
    made = pl.pallas_call(
        split_kernel,
        out_shape=shapes,
        in_specs=[vmem] * len(chunks),
        out_specs=[vmem] * len(shapes),
        compiler_params=pltpu.CompilerParams(vmem_limit_bytes=VMEM_LIMIT),
        name="split",
    )(*map(in_vmem, chunks))
    return [made[at : at + len(chunks)] for at in range(0, len(made), len(chunks))]


def join_kernel(*refs):
    size = refs[0].shape[0]
    for at, ref in enumerate(refs[:-1]):
        refs[-1][pl.ds(at * size, size)] = ref[...]


def join(parts):
    size, width = parts[0].shape
    vmem = pl.BlockSpec(memory_space=pltpu.VMEM)
    return pl.pallas_call(
        join_kernel,
        out_shape=pltpu.VMEM((size * len(parts), width), parts[0].dtype),
        in_specs=[vmem] * len(parts),
        out_specs=vmem,
        compiler_params=pltpu.CompilerParams(vmem_limit_bytes=VMEM_LIMIT),
        name="join",
    )(*map(in_vmem, parts))


def collect_kernel(panels, slots, base, *refs):
    refs, totals = refs[: -len(GROUPS)], refs[-len(GROUPS) :]
    joined, codes_ref, out_ref = refs[:-2], refs[-2], refs[-1]
    width = joined[0].shape[1]
    size = panels * slots * width + LINES
    depth = len(joined)
    parts = [joined[shift].at[pl.ds(flip * size, size)] for shift in range(depth) for flip in range(CORES)]
    col = lax.axis_index("col")
    y, core = col // CORES, lax.rem(col, CORES)
    owners = []
    for at, part in enumerate(parts):
        shift, flip = at // CORES, at % CORES
        owner = lax.rem(y + depth - shift, depth) * CORES + lax.rem(core + flip, CORES)
        owners.append(owner)
        for panel in range(panels):
            for slot in range(slots):
                out_ref[panel, owner * slots + slot] = part[pl.ds((panel * slots + slot) * width, width)]
    lines = lax.broadcasted_iota(jnp.int32, (LINES, width), 0)
    scale = jnp.zeros((LINES, width), jnp.float32)
    for at in range(panels * slots):
        scale = jnp.where(lines == at, float(base**at), scale)
    for owner, part in zip(owners, parts):
        labels = part[pl.ds(panels * slots * width, LINES), pl.ds(0, 128)].astype(jnp.float32) + 1.0
        number = jnp.sum(labels * scale[:, :128], axis=0, keepdims=True)
        digits = jnp.max(number).astype(jnp.int32)
        for panel in range(panels):
            for slot in range(slots):
                codes_ref[panel, owner * slots + slot] = lax.rem(digits, base) - 1
                digits = digits // base
    for total_ref in totals:
        total_ref[...] = jnp.zeros(total_ref.shape, jnp.float32)


def collect(parts, panels, slots, base):
    width = parts[0].shape[1]
    total = slots * CORES * len(parts)
    assert base ** (panels * slots) < 2**24
    vmem = pl.BlockSpec(memory_space=pltpu.VMEM)
    return pl.pallas_call(
        functools.partial(collect_kernel, panels, slots, base),
        out_shape=[
            pltpu.SMEM((panels, total), jnp.int32),
            pltpu.VMEM((panels, total, width, width), parts[0].dtype),
            *(pltpu.VMEM(((last - first) * width, NJ * width), jnp.float32) for first, last in GROUPS),
        ],
        in_specs=[vmem] * len(parts),
        out_specs=[pl.BlockSpec(memory_space=pltpu.SMEM)] + [vmem] * (1 + len(GROUPS)),
        compiler_params=pltpu.CompilerParams(vmem_limit_bytes=VMEM_LIMIT),
        name="collect",
    )(*map(in_vmem, parts))


def chunk_updates(codes_ref, hops, order, rows_held, slots):
    me = lax.axis_index("row")
    inverse = [order.index(at) for at in range(len(order))]
    here = pick(inverse, me)
    found = []
    for panel, way in hops:
        source = pick(order, lax.rem(here + len(order) - way, len(order)))
        owner, held = source // rows_held, lax.rem(source, rows_held)
        for at in range(slots):
            slot = owner * slots + at
            code = codes_ref[panel, slot]
            live = (code >= 0) & (code // NJ == held)
            found.append((live, slot, lax.rem(jnp.maximum(code, 0), NJ)))
    return found


def columns_of(found):
    hits = []
    for column in range(NJ):
        hit = jnp.bool_(False)
        for live, _, at in found:
            hit = hit | (live & (at == column))
        hits.append(hit)
    return hits


def fold_kernel(first, hops, later, order, rows_held, slots, band, codes_ref, ints_ref, *refs):
    chunks, rest = refs[: len(hops)], refs[len(hops) :]
    width = ints_ref.shape[2]
    found = chunk_updates(codes_ref, hops, order, rows_held, slots)
    if later is None:
        total_ref = rest[-1]
    elif later:
        total_ref, out_ref, sem = rest[-3], rest[-2], rest[-1]
        ready = [jnp.logical_not(hit) for hit in columns_of(chunk_updates(codes_ref, later, order, rows_held, slots))]
    else:
        total_ref, out_ref, sem = rest[0], rest[-2], rest[-1]
    rows = pl.ds(band[0], band[1])

    def send(column):
        cols = pl.ds(pl.multiple_of(column * width, width), width)
        return pltpu.make_async_copy(
            total_ref.at[rows, cols], out_ref.at[rows, cols], sem.at[column]
        )

    if first:
        total_ref[...] = jnp.zeros(total_ref.shape, jnp.float32)
    if later:
        hits = columns_of(found)
        for column in range(NJ):

            @pl.when(ready[column] & jnp.logical_not(hits[column]))
            def _():
                send(column).start()

    final = []
    for index, (live, slot, column) in enumerate(found):
        panel, chunk = hops[index // slots][0], chunks[index // slots]
        again = jnp.bool_(False)
        for other, _, at in found[index + 1 :]:
            again = again | (other & (at == column))
        final.append(live & jnp.logical_not(again))

        @pl.when(live)
        def _():
            cols = pl.ds(pl.multiple_of(column * width, width), width)
            total_ref[rows, cols] += jnp.dot(
                chunk[...], ints_ref[panel, slot], preferred_element_type=jnp.float32
            )

        if later is not None and not later:

            @pl.when(final[-1])
            def _():
                send(column).start()

    if later:
        for column in range(NJ):

            @pl.when(ready[column] & hits[column])
            def _():
                send(column).start()

        for column in range(NJ):

            @pl.when(ready[column])
            def _():
                send(column).wait()

    elif later is not None:
        for done, (_, _, column) in zip(final, found):

            @pl.when(done)
            def _():
                send(column).wait()


def fold(codes, ints, chunks, hops, later, total, out, order, rows_held, slots, band, whole):
    first = total is None
    rows, width = chunks[0].shape
    vmem = pl.BlockSpec(memory_space=pltpu.VMEM)
    anywhere = pl.BlockSpec(memory_space=pl.ANY)
    operands = [pltpu.with_memory_space_constraint(codes, pltpu.SMEM), in_vmem(ints), *map(in_vmem, chunks)]
    in_specs = [pl.BlockSpec(memory_space=pltpu.SMEM)] + [vmem] * (1 + len(chunks))
    aliases, scratch, out_shapes, out_specs = {}, [], [], []
    if not first:
        operands.append(in_vmem(total))
        in_specs.append(vmem)
    if later is None or later:
        if not first:
            aliases[len(operands) - 1] = 0
        out_shapes.append(pltpu.VMEM(total.shape, jnp.float32))
        out_specs.append(vmem)
    if later is not None:
        if out is not None:
            aliases[len(operands)] = len(out_shapes)
            operands.append(out)
            in_specs.append(anywhere)
        out_shapes.append(jax.ShapeDtypeStruct(whole, jnp.float32))
        out_specs.append(anywhere)
        scratch = [pltpu.SemaphoreType.DMA((NJ,))]
    return pl.pallas_call(
        functools.partial(fold_kernel, first, hops, later, order, rows_held, slots, band),
        out_shape=out_shapes,
        in_specs=in_specs,
        out_specs=out_specs,
        scratch_shapes=scratch,
        input_output_aliases=aliases,
        compiler_params=pltpu.CompilerParams(vmem_limit_bytes=VMEM_LIMIT),
        cost_estimate=pl.CostEstimate(
            flops=2 * rows * width * width * len(hops) * slots,
            bytes_accessed=rows * NJ * width * 4,
            transcendentals=0,
        ),
        name="fold",
    )(*operands)


def body(amp_tiles, amp_rows, int_tiles, int_codes):
    n_row, n_col = lax.axis_size("row"), lax.axis_size("col")
    rows_held = n_row // n_col
    panels, slots, width = int_tiles.shape[0], int_tiles.shape[1], int_tiles.shape[3]
    across = n_col // CORES
    order = grid_cycle(n_row // across, across)[::-1]
    forth = [(order[at], order[(at + 1) % n_row]) for at in range(n_row)]
    ways = [forth, [(b, a) for a, b in forth]]

    swap = [(c, c // CORES * CORES + (c + 1) % CORES) for c in range(n_col)]
    whole = (MI * width, NJ * width)
    placed = place(amp_tiles, amp_rows, int_tiles, int_codes)
    streams, parcel = placed[:-1], placed[-1]
    parts = [join([parcel, lax.ppermute(parcel, "col", swap)])]
    for shift in range(1, n_col // CORES):
        moved = lax.optimization_barrier((parts[0], parts[-1]))[0] if shift > 1 else parts[0]
        parts.append(lax.ppermute(moved, "col", [(c, (c + shift * CORES) % n_col) for c in range(n_col)]))
    codes, ints, total = collect(parts, panels, slots, rows_held * NJ + 1)
    rows = MI * width

    def add(chunks, later, total, out, band):
        tags = [tag for tag, _ in chunks]
        made = fold(
            codes, ints, [chunk for _, chunk in chunks], tags, later, total, out, order, rows_held, slots, band, whole
        )
        return made if later else made[0]

    far = n_row // 2
    lead = [(panel % 2, panel) for panel in range(panels)]
    rest = [(1 - panel % 2, panel) for panel in range(panels)]

    def tag(way, panel, hop):
        return (panel, hop if way == 0 else n_row - hop)

    held = {(way, panel): streams[panel] for way in range(2) for panel in range(panels)}
    have = [((panel, 0), streams[panel]) for panel in range(panels)]
    for hop in range(1, far):
        if hop == far - 1:
            total = early = add(have, None, total, None, (0, rows))
            have = []
        for one in lead + rest:
            if hop < far - 1 or far - 1 <= n_row - 1 - far or one in lead:
                held[one] = lax.ppermute(held[one], "row", ways[one[0]])
                have.append((tag(*one, hop), held[one]))
    last = [held[one] for one in lead]
    pieces = split(last)
    later = [tag(*one, far) for one in lead]
    ends = [[lax.ppermute(part, "row", ways[one[0]]) for one, part in zip(lead, piece)] for piece in pieces]
    total, out = add(have, later, total, None, (0, rows))
    first = 0
    for piece, eighths in zip(ends, PIECES):
        out = add(list(zip(later, piece)), [], total, out, (first, rows * eighths // 8))
        first += rows * eighths // 8
    return out


def solution(mesh):
    return jax.shard_map(
        body,
        mesh=mesh,
        in_specs=(
            P(None, "col", "row", None, None),
            P(None, "col", "row"),
            P(None, "col", "row", None, None),
            P(None, "col", "row"),
        ),
        out_specs=P("col", "row"),
        check_vma=False,
    )
```
